128 devices in a mesh: dp: 8 (over x, y_lo), ctx: 16 (over y_hi, z, core).
Axes of the slice: x: 4, y: 4 (y_hi: 2, y_lo: 2; y = y_hi * 2 + y_lo), z: 4, core: 2. Of those that a mesh axis runs over, the one named last changes fastest.
Arguments:
- hyena_q: bfloat16 [16384, 4096], P(('dp', 'ctx')), parts along dimension 0, may hold values from -6 to 6
- hyena_k: bfloat16 [16384, 4096], P(('dp', 'ctx')), parts along dimension 0, may hold values from -6 to 6
- hyena_v: bfloat16 [16384, 4096], P(('dp', 'ctx')), parts along dimension 0, may hold values from -6 to 6
- short_filter: float32 [3, 3, 4096], replicated, may hold values from -3.5 to 3.5
- residue: float32 [4096, 16], P('ctx'), may hold values from -0.0625 to 0.0625
- decay_rate: float32 [4096, 16], P('ctx'), may hold values from 0.00012207031 to 0.034
- att_query: bfloat16 [16384, 4096], P(('dp', 'ctx')), parts along dimension 0, may hold values from -32 to 32
- att_key: bfloat16 [16384, 4096], P(('dp', 'ctx')), parts along dimension 0, may hold values from -6 to 6
- att_value: bfloat16 [16384, 4096], P(('dp', 'ctx')), parts along dimension 0, may hold values from -6 to 6
Outputs:
- hyena_out: bfloat16 [16384, 4096], P(('dp', 'ctx')), parts along dimension 0
- att_out: bfloat16 [16384, 4096], P(('dp', 'ctx')), parts along dimension 0
The draws below stay inside these ranges and needn't reach their ends.
There are 8 independent parts, one for each index of `dp`. The reference program is written for one: setup_inputs(seed, part) draws one part's arguments, and reference() takes and returns one part's arrays. A program takes and returns all parts, laid end to end along the dimension named above; an argument that names none is the same for every part. Nothing has to cross between parts.
All inputs are finite; a program needn't handle non-finite values.
Results may differ from the reference program's by a relative error of at most 0.0058.
Values may be sent and summed in bfloat16 or wider, within the bound.
A program may use at most 128 MiB of HBM per device.

```python
import math
import jax
import jax.numpy as jnp
from jax import lax

D = 4096
HEADS = 32
HEAD_DIM = 128
ORDER = 16
TAPS = 3
SEQ = 2048


def draw_att_query(key, part):
    key = jax.random.fold_in(key, 11)
    return jnp.clip(jax.random.normal(key, (SEQ, D), jnp.float32), -6.0, 6.0).astype(jnp.bfloat16)


def draw_att_key(key, part):
    key = jax.random.fold_in(key, 12)
    return jnp.clip(jax.random.normal(key, (SEQ, D), jnp.float32), -6.0, 6.0).astype(jnp.bfloat16)


def draw_decay_rate(key, part):
    key = jax.random.fold_in(key, 13)
    lowest = 0.5 / SEQ
    highest = 1.0 / 30.0
    uniform_draw = jax.random.uniform(key, (D, ORDER), jnp.float32)
    return jnp.exp(math.log(lowest) + (math.log(highest) - math.log(lowest)) * uniform_draw)


def block_scale(stream_key, shape, pieces, least, high):
    def one(dim, parts):
        steps = jax.random.uniform(jax.random.fold_in(jax.random.fold_in(stream_key, 6), dim), (parts,), jnp.float32, least / len(pieces), high / len(pieces))
        return jnp.repeat(jnp.exp(steps), shape[dim] // parts).reshape((-1,) + (1,) * (len(shape) - dim - 1))

    factor_of = one(*pieces[0])
    for cut in pieces[1:]:
        factor_of = factor_of * one(*cut)
    return factor_of


def centred(own_key, dims, spread, reach, split=(), kind=jnp.bfloat16):
    drawn = spread * jax.random.normal(own_key, dims, jnp.float32)
    if split:
        drawn = drawn * block_scale(own_key, dims, split, -0.22, 0.18)
    return jnp.clip(drawn, -reach, reach).astype(kind)


def setup_inputs(seed: int = 0, part: int = 0) -> dict:
    key_of = jax.random.split(jax.random.key(seed), 10)
    part_splits = jax.random.split(jax.random.fold_in(key_of[9], part), 10)
    return {
        "hyena_q": centred(part_splits[0], (SEQ, D), 1.0, 6.0, ((0, 16),)),
        "hyena_k": centred(part_splits[1], (SEQ, D), 1.0, 6.0, ((0, 16),)),
        "hyena_v": centred(part_splits[2], (SEQ, D), 1.0, 6.0, ((0, 16),)),
        "short_filter": centred(key_of[3], (3, TAPS, D), 0.6, 3.5, (), jnp.float32),
        "residue": centred(key_of[4], (D, ORDER), (2.0 / (ORDER * SEQ) ** 0.5), 0.0625, ((0, 16),), jnp.float32),
        "decay_rate": draw_decay_rate(jax.random.fold_in(key_of[9], 71), part),
        "att_query": draw_att_query(jax.random.fold_in(jax.random.fold_in(key_of[9], part), 71), part),
        "att_key": draw_att_key(jax.random.fold_in(jax.random.fold_in(key_of[9], part), 71), part),
        "att_value": centred(part_splits[8], (SEQ, D), 1.0, 6.0, ((0, 16),)),
    }


def short_mix(feature, tap_weights):
    values = feature.astype(jnp.float32)
    padded = jnp.concatenate([jnp.zeros((TAPS - 1, values.shape[1]), jnp.float32), values], 0)
    length = values.shape[0]
    result = tap_weights[0] * padded[TAPS - 1:TAPS - 1 + length]
    for offset in range(1, TAPS):
        result = result + tap_weights[offset] * padded[TAPS - 1 - offset:TAPS - 1 - offset + length]
    return result


def long_kernel(residue, decay_rate, length):
    time_index = jnp.arange(length, dtype=jnp.float32)[:, None]
    kernel = jnp.zeros((length, residue.shape[0]), jnp.float32)
    for mode_index in range(ORDER):
        kernel = kernel + residue[:, mode_index] * jnp.exp(-decay_rate[:, mode_index] * time_index)
    return kernel


def one_head(items):
    query_head, key_head, value_head = items
    scores = jnp.dot(query_head, key_head.T, preferred_element_type=jnp.float32) * (HEAD_DIM ** -0.5)
    row_pos = jnp.arange(SEQ, dtype=jnp.int32)[:, None]
    col_pos = jnp.arange(SEQ, dtype=jnp.int32)[None, :]
    scores = jnp.where(col_pos <= row_pos, scores, -jnp.inf)
    row_top = jnp.max(scores, axis=1, keepdims=True)
    expo = jnp.exp(scores - row_top)
    denominator = jnp.sum(expo, axis=1)
    weights = expo.astype(jnp.bfloat16)
    mixed_out = jnp.dot(weights, value_head, preferred_element_type=jnp.float32) / denominator[:, None]
    return mixed_out.astype(jnp.bfloat16)


def reference(hyena_q, hyena_k, hyena_v, short_filter, residue, decay_rate, att_query, att_key, att_value):
    query_mix = short_mix(hyena_q, short_filter[0])
    key_mix = short_mix(hyena_k, short_filter[1])
    value_mix = short_mix(hyena_v, short_filter[2])
    product = lax.optimization_barrier((key_mix * value_mix).astype(jnp.bfloat16))
    kernel = long_kernel(residue, decay_rate, SEQ)
    spectrum = jnp.fft.rfft(product.astype(jnp.float32), n=2 * SEQ, axis=0) * jnp.fft.rfft(kernel, n=2 * SEQ, axis=0)
    smoothed = jnp.fft.irfft(spectrum, n=2 * SEQ, axis=0)[:SEQ].astype(jnp.bfloat16)
    smoothed = lax.optimization_barrier(smoothed)
    hyena_out = (query_mix * smoothed.astype(jnp.float32)).astype(jnp.bfloat16)

    def by_heads(matrix):
        return matrix.reshape(SEQ, HEADS, HEAD_DIM).transpose(1, 0, 2)

    heads = lax.map(one_head, (by_heads(att_query), by_heads(att_key), by_heads(att_value)))
    att_out = heads.transpose(1, 0, 2).reshape(SEQ, D)
    return (hyena_out, att_out)
```

```python
import functools
import math

import jax
import jax.numpy as jnp
from jax import lax
from jax.experimental import pallas as pl
from jax.experimental.pallas import tpu as pltpu
from jax.sharding import PartitionSpec as P

MESH = pl.DeviceIdType.MESH
f32, bf16 = jnp.float32, jnp.bfloat16

N = 16
ROWS = 128
SEQ = N * ROWS
D = 4096
MODES = 16
HEAD = 128
HEADS = D // HEAD // N
QBLOCK = 256
EXP2_SCALE = HEAD**-0.5 * math.log2(math.e)
STATE = MODES * 2


def row_of(j):
    return j % 2 * 16 + j // 2


def total(terms):
    while len(terms) > 1:
        terms = [a + b for a, b in zip(terms[::2], terms[1::2])]
    return terms[0]


def attend(q_ref, k_ref, v_ref, o_ref, block):
    end = (block + 1) * QBLOCK
    start = end - QBLOCK
    scores = lax.dot_general(
        q_ref[start:end, :], k_ref[:end, :], (((1,), (1,)), ((), ())), preferred_element_type=f32
    )
    row = lax.broadcasted_iota(jnp.int32, (QBLOCK, QBLOCK), 0)
    col = lax.broadcasted_iota(jnp.int32, (QBLOCK, QBLOCK), 1)
    diagonal = jnp.where(col <= row, scores[:, start:], -jnp.inf)
    top = jnp.max(diagonal, axis=1, keepdims=True)
    if block:
        top = jnp.maximum(top, jnp.max(scores[:, :start], axis=1, keepdims=True))
        scores = jnp.concatenate([scores[:, :start], diagonal], axis=1)
    else:
        scores = diagonal
    expo = jnp.exp2((scores - top) * EXP2_SCALE)
    denominator = jnp.sum(expo, axis=1, keepdims=True)
    mixed = jnp.dot(expo.astype(bf16), v_ref[:end, :], preferred_element_type=f32)
    o_ref[start:end, :] = (mixed / denominator).astype(bf16)


def short_filters(hx, halo, taps, qs, product, shifted):
    def column(j, carry):
        cs = pl.ds(pl.multiple_of(j * 128, 128), 128)

        def mix(f):
            x = hx[f, :, cs].astype(f32)
            shifted[f, 8 : 8 + ROWS, :] = x
            shifted[f, 6:8, :] = halo[2 * f : 2 * f + 2, cs]
            w = taps[f, :, cs]
            return (
                w[0:1] * x + w[1:2] * shifted[f, 7 : 7 + ROWS, :] + w[2:3] * shifted[f, 6 : 6 + ROWS, :]
            )

        qs[:, cs] = mix(0)
        both = (mix(1) * mix(2)).astype(bf16).astype(f32)
        product[pl.ds(row_of(j), ROWS, stride=32), :] = both
        return carry

    lax.fori_loop(0, D // 128, column, 0)


def mode_rows(ref, g, n, per_owner, first=0):
    return pl.ds(g % 2 * 8 * per_owner + first + n * 2 + g // 2, 8, stride=per_owner)


def scan(params, product, smooth, states):
    for g in range(4):
        power = [params[mode_rows(params, g, n, 2 * STATE), :] for n in range(MODES)]
        weight = [params[mode_rows(params, g, n, 2 * STATE, STATE), :] for n in range(MODES)]

        def step(t, state):
            rows = pl.ds(pl.multiple_of(t * 32 + g * 8, 8), 8)
            x = product[rows, :]
            state = [h * p + x for h, p in zip(state, power)]
            smooth[rows, :] = total([h * w for h, w in zip(state, weight)])
            return state

        state = lax.fori_loop(0, ROWS, step, [jnp.zeros((8, 128), f32)] * MODES, unroll=4)
        for n in range(MODES):
            states[mode_rows(states, g, n, STATE), :] = state[n]


def add_carried(params, carried, smooth):
    for g in range(4):
        power = [params[mode_rows(params, g, n, 2 * STATE), :] for n in range(MODES)]
        first = [
            params[mode_rows(params, g, n, 2 * STATE, STATE), :]
            * power[n]
            * carried[mode_rows(carried, g, n, STATE), :]
            for n in range(MODES)
        ]

        def step(t, term):
            rows = pl.ds(pl.multiple_of(t * 32 + g * 8, 8), 8)
            smooth[rows, :] = smooth[rows, :] + total(term)
            return [a * p for a, p in zip(term, power)]

        lax.fori_loop(0, ROWS, step, first, unroll=4)


def gate(smooth, qs, out):
    def column(j, carry):
        cs = pl.ds(pl.multiple_of(j * 128, 128), 128)
        y = smooth[pl.ds(row_of(j), ROWS, stride=32), :]
        out[:, cs] = (qs[:, cs] * y.astype(bf16).astype(f32)).astype(bf16)
        return carry

    lax.fori_loop(0, D // 128, column, 0, unroll=4)


def kernel(
    hq, hk, hv, taps_in, residue_in, decay_in, aq, ak, av,
    hyena_out, att_out,
    hx, taps, residue, decay, edge, halo, mine, params, leap, qs, product, smooth, shifted,
    ends, gathered, chained, carried, qkv, mixed, gated,
    load_sem, own_sem, out_sem,
    halo_s, halo_r, par_s, par_r, end_s, end_r, cha_s, cha_r, qkv_s, qkv_r, mix_s, mix_r,
):
    me = lax.axis_index("ctx")

    def moved(d, sign):
        z = (me // 2 + sign * (d // 2 % 4) + 4) % 4
        return (me // 8 + d // 8) % 2 * 8 + z * 2 + (me + d) % 2

    def target(d):
        return moved(d, 1)

    def source(d):
        return moved(d, -1)

    def each_peer(do):
        def step(d, carry):
            do(d)
            return carry

        lax.fori_loop(1, N, step, 0)

    def rows(p, count):
        return pl.ds(pl.multiple_of(p * count, count), count)

    def columns(p, h):
        return pl.ds(pl.multiple_of((p * HEADS + h) * HEAD, HEAD), HEAD)

    def remote(src, dst, send, recv, device):
        return pltpu.make_async_remote_copy(
            src_ref=src, dst_ref=dst, send_sem=send, recv_sem=recv,
            device_id={"ctx": device}, device_id_type=MESH,
        )

    loads = [
        pltpu.make_async_copy(src, dst, load_sem.at[i])
        for i, (src, dst) in enumerate(
            [(residue_in, residue), (decay_in, decay), (taps_in, taps)]
            + [(x, hx.at[f]) for f, x in enumerate((hq, hk, hv))]
        )
    ]
    for copy in loads:
        copy.start()

    barrier = pltpu.get_barrier_semaphore()
    each_peer(
        lambda d: pl.semaphore_signal(barrier, inc=1, device_id={"ctx": target(d)}, device_id_type=MESH)
    )

    att = (aq, ak, av)
    own = [
        [pltpu.make_async_copy(att[t].at[:, columns(me, h)], qkv.at[h, t, rows(me, ROWS)], own_sem.at[h, t]) for t in range(3)]
        for h in range(HEADS)
    ]
    for h in range(HEADS):
        for copy in own[h]:
            copy.start()

    loads[0].wait()
    loads[1].wait()
    rate = decay[...]
    weight = residue[...]
    for half in range(2):
        cs = slice(half * 128, half * 128 + 128)
        mine[pl.ds(half, MODES, stride=2), :] = jnp.exp(-rate[:, cs])
        mine[pl.ds(STATE + half, MODES, stride=2), :] = weight[:, cs]
        leap[pl.ds(half, MODES, stride=2), :] = jnp.exp(-(rate[:, cs] * float(ROWS)))
    params[rows(me, 2 * STATE), :] = mine[...]
    for copy in loads[2:]:
        copy.wait()
    edge[...] = jnp.zeros_like(edge)
    for f in range(3):
        edge[2 * f : 2 * f + 2, :] = hx[f, ROWS - 16 : ROWS, :].astype(f32)[14:16]

    pl.semaphore_wait(barrier, N - 1)

    halo_copy = remote(edge, halo, halo_s, halo_r, (me + 1) % N)
    halo_copy.start()

    def par_copy(d, p):
        return remote(mine, params.at[rows(p, 2 * STATE)], par_s.at[d], par_r.at[d], target(d))

    def qkv_copy(h, t, d, p):
        return remote(
            att[t].at[:, columns(target(d), h)], qkv.at[h, t, rows(p, ROWS)],
            qkv_s.at[h, t, d], qkv_r.at[h, t, d], target(d),
        )

    def end_copy(d, p):
        return remote(ends.at[rows(target(d), STATE)], gathered.at[rows(p, STATE)], end_s.at[d], end_r.at[d], target(d))

    def cha_copy(d, p):
        return remote(chained.at[rows(target(d), STATE)], carried.at[rows(p, STATE)], cha_s.at[d], cha_r.at[d], target(d))

    def mix_copy(h, d, p):
        return remote(
            mixed.at[h, rows(target(d), ROWS)], att_out.at[:, columns(p, h)],
            mix_s.at[h, d], mix_r.at[h, d], target(d),
        )

    def qkv_start(h):
        def one(d):
            for t in range(3):
                qkv_copy(h, t, d, me).start()

        each_peer(one)

    def qkv_wait(h):
        def one(d):
            for t in range(3):
                qkv_copy(h, t, d, source(d)).wait_recv()

        each_peer(one)
        for copy in own[h]:
            copy.wait()

    each_peer(lambda d: par_copy(d, me).start())
    qkv_start(0)

    halo_copy.wait_recv()

    @pl.when(me == 0)
    def _():
        halo[...] = jnp.zeros_like(halo)

    short_filters(hx, halo, taps, qs, product, shifted)
    each_peer(lambda d: par_copy(d, source(d)).wait_recv())
    scan(params, product, smooth, ends)
    gathered[rows(me, STATE), :] = ends[rows(me, STATE), :]
    each_peer(lambda d: end_copy(d, me).start())
    qkv_start(1)

    def attention(h):
        qkv_wait(h)
        for block in range(SEQ // QBLOCK):
            attend(qkv.at[h, 0], qkv.at[h, 1], qkv.at[h, 2], mixed.at[h], block)
        each_peer(lambda d: mix_copy(h, d, me).start())
        copy = pltpu.make_async_copy(mixed.at[h, rows(me, ROWS)], att_out.at[:, columns(me, h)], out_sem.at[h])
        copy.start()
        return copy

    kept = [attention(0)]

    each_peer(lambda d: end_copy(d, source(d)).wait_recv())

    def chain(p, state):
        chained[rows(p, STATE), :] = state
        return state * leap[...] + gathered[rows(p, STATE), :]

    lax.fori_loop(0, N, chain, jnp.zeros((STATE, 128), f32))
    carried[rows(me, STATE), :] = chained[rows(me, STATE), :]
    each_peer(lambda d: cha_copy(d, me).start())

    kept.append(attention(1))

    each_peer(lambda d: cha_copy(d, source(d)).wait_recv())
    add_carried(params, carried, smooth)
    gate(smooth, qs, gated)
    last = pltpu.make_async_copy(gated, hyena_out, out_sem.at[2])
    last.start()

    halo_copy.wait_send()

    def finish(d):
        par_copy(d, me).wait_send()
        end_copy(d, me).wait_send()
        cha_copy(d, me).wait_send()
        for h in range(HEADS):
            for t in range(3):
                qkv_copy(h, t, d, me).wait_send()
            mix_copy(h, d, me).wait_send()
            mix_copy(h, d, source(d)).wait_recv()

    each_peer(finish)
    for copy in kept:
        copy.wait()
    last.wait()


def local(hyena_q, hyena_k, hyena_v, short_filter, residue, decay_rate, att_query, att_key, att_value):
    residue, decay_rate = residue.T, decay_rate.T
    vmem = pltpu.VMEM
    dma = pltpu.SemaphoreType.DMA
    return pl.pallas_call(
        kernel,
        out_shape=(jax.ShapeDtypeStruct((ROWS, D), bf16), jax.ShapeDtypeStruct((ROWS, D), bf16)),
        in_specs=[pl.BlockSpec(memory_space=pltpu.HBM)] * 9,
        out_specs=(pl.BlockSpec(memory_space=pl.ANY), pl.BlockSpec(memory_space=pl.ANY)),
        scratch_shapes=[
            vmem((3, ROWS, D), bf16),
            vmem(short_filter.shape, f32),
            vmem(residue.shape, f32),
            vmem(decay_rate.shape, f32),
            vmem((8, D), f32),
            vmem((8, D), f32),
            vmem((2 * STATE, 128), f32),
            vmem((N * 2 * STATE, 128), f32),
            vmem((STATE, 128), f32),
            vmem((ROWS, D), f32),
            vmem((ROWS * 32, 128), f32),
            vmem((ROWS * 32, 128), f32),
            vmem((3, ROWS + 8, 128), f32),
            vmem((N * STATE, 128), f32),
            vmem((N * STATE, 128), f32),
            vmem((N * STATE, 128), f32),
            vmem((N * STATE, 128), f32),
            vmem((HEADS, 3, SEQ, HEAD), bf16),
            vmem((HEADS, SEQ, HEAD), bf16),
            vmem((ROWS, D), bf16),
            dma((6,)),
            dma((HEADS, 3)),
            dma((3,)),
            dma,
            dma,
            dma((N,)),
            dma((N,)),
            dma((N,)),
            dma((N,)),
            dma((N,)),
            dma((N,)),
            dma((HEADS, 3, N)),
            dma((HEADS, 3, N)),
            dma((HEADS, N)),
            dma((HEADS, N)),
        ],
        compiler_params=pltpu.CompilerParams(
            collective_id=0, has_side_effects=True, vmem_limit_bytes=63 * 2**20
        ),
    )(hyena_q, hyena_k, hyena_v, short_filter, residue, decay_rate, att_query, att_key, att_value)


def solution(mesh):
    rows = P(("dp", "ctx"), None)
    placed = (rows, rows, rows, P(), P("ctx", None), P("ctx", None), rows, rows, rows)
    return jax.shard_map(local, mesh=mesh, in_specs=placed, out_specs=(rows, rows), check_vma=False)
```

```python
import functools
import math

import jax
import jax.numpy as jnp
from jax import lax
from jax.experimental import pallas as pl
from jax.experimental.pallas import tpu as pltpu
from jax.sharding import PartitionSpec as P

MESH = pl.DeviceIdType.MESH
f32, bf16 = jnp.float32, jnp.bfloat16

N = 16
CHIPS = N // 2
NEAR = CHIPS + 2
ROWS = 128
SEQ = N * ROWS
D = 4096
MODES = 16
HEAD = 128
HEADS = D // HEAD // N
QBLOCK = 256
EXP2_SCALE = HEAD**-0.5 * math.log2(math.e)
STATE = MODES * 2


def row_of(j):
    return j % 2 * 16 + j // 2 % 2 * 8 + j // 4


def total(terms):
    while len(terms) > 1:
        terms = [a + b for a, b in zip(terms[::2], terms[1::2])]
    return terms[0]


def attend(q_ref, k_ref, v_ref, o_ref, block):
    end = (block + 1) * QBLOCK
    start = end - QBLOCK
    scores = lax.dot_general(
        q_ref[start:end, :], k_ref[:end, :], (((1,), (1,)), ((), ())), preferred_element_type=f32
    )
    row = lax.broadcasted_iota(jnp.int32, (QBLOCK, QBLOCK), 0)
    col = lax.broadcasted_iota(jnp.int32, (QBLOCK, QBLOCK), 1)
    diagonal = jnp.where(col <= row, scores[:, start:], -jnp.inf)
    top = jnp.max(diagonal, axis=1, keepdims=True)
    if block:
        top = jnp.maximum(top, jnp.max(scores[:, :start], axis=1, keepdims=True))
        scores = jnp.concatenate([scores[:, :start], diagonal], axis=1)
    else:
        scores = diagonal
    expo = jnp.exp2((scores - top) * EXP2_SCALE)
    denominator = jnp.sum(expo, axis=1, keepdims=True)
    mixed = jnp.dot(expo.astype(bf16), v_ref[:end, :], preferred_element_type=f32)
    o_ref[start:end, :] = (mixed / denominator).astype(bf16)


def edge_at(j, f, r):
    return pl.ds(j * 6 + 2 * f + r, 1)


def pack_edge(hx, wide):
    def column(j, carry):
        cs = pl.ds(pl.multiple_of(j * 128, 128), 128)
        for f in range(3):
            last = hx[f, ROWS - 16 : ROWS, cs].astype(f32)
            for r in range(2):
                wide[edge_at(j, f, r), :] = last[14 + r : 15 + r]
        return carry

    lax.fori_loop(0, D // 128, column, 0)


def short_filters(hx, halo, taps, qs, product, shifted):
    def column(j, carry):
        cs = pl.ds(pl.multiple_of(j * 128, 128), 128)

        def mix(f):
            x = hx[f, :, cs].astype(f32)
            shifted[f, 8 : 8 + ROWS, :] = x
            for r in range(2):
                shifted[f, 6 + r : 7 + r, :] = halo[edge_at(j, f, r), :]
            w = taps[f, :, cs]
            return (
                w[0:1] * x + w[1:2] * shifted[f, 7 : 7 + ROWS, :] + w[2:3] * shifted[f, 6 : 6 + ROWS, :]
            )

        qs[:, cs] = mix(0)
        both = (mix(1) * mix(2)).astype(bf16).astype(f32)
        product[pl.ds(row_of(j), ROWS, stride=32), :] = both
        return carry

    lax.fori_loop(0, D // 128, column, 0)


def mode_rows(ref, g, n, per_owner, first=0):
    return pl.ds(g % 2 * 8 * per_owner + first + n * 2 + g // 2, 8, stride=per_owner)


def scan(params, product, smooth, states):
    for g in range(4):
        power = [params[mode_rows(params, g, n, 2 * STATE), :] for n in range(MODES)]
        weight = [params[mode_rows(params, g, n, 2 * STATE, STATE), :] for n in range(MODES)]

        def step(t, state):
            rows = pl.ds(pl.multiple_of(t * 32 + g * 8, 8), 8)
            x = product[rows, :]
            state = [h * p + x for h, p in zip(state, power)]
            smooth[rows, :] = total([h * w for h, w in zip(state, weight)])
            return state

        state = lax.fori_loop(0, ROWS, step, [jnp.zeros((8, 128), f32)] * MODES, unroll=4)
        for n in range(MODES):
            states[mode_rows(states, g, n, STATE), :] = state[n]


def add_carried(params, carried, smooth):
    for g in range(4):
        power = [params[mode_rows(params, g, n, 2 * STATE), :] for n in range(MODES)]
        first = [
            params[mode_rows(params, g, n, 2 * STATE, STATE), :]
            * power[n]
            * carried[mode_rows(carried, g, n, STATE), :]
            for n in range(MODES)
        ]

        def step(t, term):
            rows = pl.ds(pl.multiple_of(t * 32 + g * 8, 8), 8)
            smooth[rows, :] = smooth[rows, :] + total(term)
            return [a * p for a, p in zip(term, power)]

        lax.fori_loop(0, ROWS, step, first, unroll=4)


def gate(smooth, qs, out):
    def column(j, carry):
        cs = pl.ds(pl.multiple_of(j * 128, 128), 128)
        y = smooth[pl.ds(row_of(j), ROWS, stride=32), :]
        out[:, cs] = (qs[:, cs] * y.astype(bf16).astype(f32)).astype(bf16)
        return carry

    lax.fori_loop(0, D // 128, column, 0, unroll=4)


def kernel(
    hq, hk, hv, taps_in, residue_in, decay_in, aq, ak, av,
    hyena_out, att_out,
    hx, taps, residue, decay, wide, edge, halo, mine, params, leap, step, qs, product, smooth, shifted,
    ends, pair, joint, gathered, chained, start, beside, carried, qkv, mixed, gated,
    ready, load_sem, own_sem, out_sem, one_s, one_r,
    par_s, par_r, end_s, end_r, cha_s, cha_r, qkv_s, qkv_r, mix_s, mix_r,
):
    me = lax.axis_index("ctx")
    core = me % 2
    chip = me // 2
    other = me + 1 - 2 * core

    def moved(d, sign):
        z = (me // 2 + sign * (d // 2 % 4) + 4) % 4
        return (me // 8 + d // 8) % 2 * 8 + z * 2 + (me + d) % 2

    def target(d):
        return moved(d, 1)

    def source(d):
        return moved(d, -1)

    def each_peer(do, last_first=False, begin=1, end=N):
        def at(d, carry):
            do(begin + end - 1 - d if last_first else d)
            return carry

        lax.fori_loop(begin, end, at, 0)

    def each_chip(do, begin=1, end=CHIPS):
        def at(e, carry):
            do(2 * e)
            return carry

        lax.fori_loop(begin, end, at, 0)

    def rows(p, count):
        return pl.ds(pl.multiple_of(p * count, count), count)

    def columns(p, h):
        return pl.ds(pl.multiple_of((p * HEADS + h) * HEAD, HEAD), HEAD)

    def remote(src, dst, send, recv, device):
        return pltpu.make_async_remote_copy(
            src_ref=src, dst_ref=dst, send_sem=send, recv_sem=recv,
            device_id={"ctx": device}, device_id_type=MESH,
        )

    loads = [
        pltpu.make_async_copy(src, dst, load_sem.at[i])
        for i, (src, dst) in enumerate(
            [(residue_in, residue), (decay_in, decay), (taps_in, taps)]
            + [(x, hx.at[f]) for f, x in enumerate((hq, hk, hv))]
        )
    ]

    barrier = pltpu.get_barrier_semaphore()
    each_peer(
        lambda d: pl.semaphore_signal(barrier, inc=1, device_id={"ctx": target(d)}, device_id_type=MESH),
        last_first=True,
        end=NEAR,
    )
    for copy in loads:
        copy.start()

    att = (aq, ak, av)
    own = [
        [
            pltpu.make_async_copy(att[t].at[:, columns(me, h)], qkv.at[h, t, rows(me, ROWS)], own_sem.at[h, t])
            for t in range(3)
        ]
        for h in range(HEADS)
    ]
    for h in range(HEADS):
        for copy in own[h]:
            copy.start()

    loads[0].wait()
    loads[1].wait()
    rate = decay[...]
    weight = residue[...]
    for half in range(2):
        cs = slice(half * 128, half * 128 + 128)
        mine[pl.ds(half, MODES, stride=2), :] = jnp.exp(-rate[:, cs])
        mine[pl.ds(STATE + half, MODES, stride=2), :] = weight[:, cs]
        leap[pl.ds(half, MODES, stride=2), :] = jnp.exp(-(rate[:, cs] * float(2 * ROWS)))
    slot = core * CHIPS + chip
    params[rows(slot, 2 * STATE), :] = mine[...]
    for copy in loads[2:]:
        copy.wait()
    pack_edge(hx, wide)
    edge[...] = wide[...].astype(bf16)

    pl.semaphore_wait(barrier, NEAR - 1)
    pl.semaphore_signal(ready, inc=1, device_id={"ctx": target(N // 2)}, device_id_type=MESH)

    halo_copy = remote(edge, halo, one_s.at[0], one_r.at[0], (me + 1) % N)
    half_rows = CHIPS * 2 * STATE
    par_on = remote(
        params.at[rows(core, half_rows)], params.at[rows(core, half_rows)], one_s.at[1], one_r.at[1], other
    )
    end_on = remote(ends.at[rows(1 - core, CHIPS * STATE)], pair, one_s.at[2], one_r.at[2], other)
    cha_on = remote(beside, carried.at[rows(core, CHIPS * STATE)], one_s.at[3], one_r.at[3], other)

    def par_copy(d, p):
        return remote(
            mine, params.at[rows(core * CHIPS + p // 2, 2 * STATE)], par_s.at[d // 2], par_r.at[d // 2], target(d)
        )

    def end_copy(d, p):
        return remote(
            joint.at[rows(target(d) // 2, STATE)], gathered.at[rows(p // 2, STATE)],
            end_s.at[d // 2], end_r.at[d // 2], target(d),
        )

    def cha_copy(d, p):
        return remote(
            chained.at[rows(target(d) // 2, STATE)], start.at[rows(p // 2, STATE)],
            cha_s.at[d // 2], cha_r.at[d // 2], target(d),
        )

    def qkv_copy(h, t, d, p):
        return remote(
            att[t].at[:, columns(target(d), h)], qkv.at[h, t, rows(p, ROWS)],
            qkv_s.at[h, t, d], qkv_r.at[h, t, d], target(d),
        )

    def mix_copy(h, d, p):
        return remote(
            mixed.at[h, rows(target(d), ROWS)], att_out.at[:, columns(p, h)],
            mix_s.at[h, d], mix_r.at[h, d], target(d),
        )

    def qkv_start(h, tensors, begin=1, end=N):
        def one(d):
            for t in tensors:
                qkv_copy(h, t, d, me).start()

        each_peer(one, last_first=True, begin=begin, end=end)

    def qkv_wait(h):
        def one(d):
            for t in range(3):
                qkv_copy(h, t, d, source(d)).wait_recv()

        each_peer(one)
        for copy in own[h]:
            copy.wait()

    each_chip(lambda d: par_copy(d, me).start(), 1, CHIPS // 2 + 1)
    qkv_start(0, (0,), end=NEAR)
    pl.semaphore_wait(ready, 1)
    each_chip(lambda d: par_copy(d, me).start(), CHIPS // 2 + 1, CHIPS)

    @pl.when(me < N - 1)
    def _():
        halo_copy.start()

    qkv_start(0, (0,), begin=NEAR)
    qkv_start(0, (1, 2))

    @pl.when(me > 0)
    def _():
        halo_copy.wait_recv()
        wide[...] = halo[...].astype(f32)

    @pl.when(me == 0)
    def _():
        wide[...] = jnp.zeros_like(wide)

    short_filters(hx, wide, taps, qs, product, shifted)
    each_chip(lambda d: par_copy(d, source(d)).wait_recv())
    par_on.start()
    par_on.wait_recv()
    scan(params, product, smooth, ends)
    end_on.start()

    for p in range(CHIPS):
        power = params[pl.ds(pl.multiple_of(core * half_rows + p * 2 * STATE, STATE), STATE), :]
        for _ in range(7):
            power = power * power
        step[p * STATE : (p + 1) * STATE, :] = power

    end_on.wait_recv()
    same = ends[rows(core, CHIPS * STATE), :]
    first = jnp.where(core == 0, same, pair[...])
    joint[...] = first * step[...] + jnp.where(core == 0, pair[...], same)
    gathered[rows(chip, STATE), :] = joint[rows(chip, STATE), :]
    each_chip(lambda d: end_copy(d, me).start())
    qkv_start(1, (0, 1, 2))

    def attention(h):
        qkv_wait(h)
        for block in range(SEQ // QBLOCK):
            attend(qkv.at[h, 0], qkv.at[h, 1], qkv.at[h, 2], mixed.at[h], block)

    def mix_start(h):
        each_peer(lambda d: mix_copy(h, d, me).start(), last_first=True)
        copy = pltpu.make_async_copy(mixed.at[h, rows(me, ROWS)], att_out.at[:, columns(me, h)], out_sem.at[h])
        copy.start()
        return copy

    attention(0)

    each_chip(lambda d: end_copy(d, source(d)).wait_recv())

    def chain(p, state):
        chained[rows(p, STATE), :] = state
        return state * leap[...] + gathered[rows(p, STATE), :]

    lax.fori_loop(0, CHIPS, chain, jnp.zeros((STATE, 128), f32))
    start[rows(chip, STATE), :] = chained[rows(chip, STATE), :]
    each_chip(lambda d: cha_copy(d, me).start())

    kept = [mix_start(0)]

    attention(1)
    kept.append(mix_start(1))

    each_chip(lambda d: cha_copy(d, source(d)).wait_recv())
    same = ends[rows(core, CHIPS * STATE), :]
    first = jnp.where(core == 0, same, pair[...])
    even = start[...]
    odd = even * step[...] + first
    carried[rows(core, CHIPS * STATE), :] = jnp.where(core == 0, even, odd)
    beside[...] = jnp.where(core == 0, odd, even)
    cha_on.start()
    cha_on.wait_recv()
    add_carried(params, carried, smooth)
    gate(smooth, qs, gated)
    last = pltpu.make_async_copy(gated, hyena_out, out_sem.at[2])
    last.start()

    @pl.when(me < N - 1)
    def _():
        halo_copy.wait_send()

    for copy in (par_on, end_on, cha_on):
        copy.wait_send()

    def chips_done(d):
        par_copy(d, me).wait_send()
        end_copy(d, me).wait_send()
        cha_copy(d, me).wait_send()

    def peers_done(d):
        for h in range(HEADS):
            for t in range(3):
                qkv_copy(h, t, d, me).wait_send()
            mix_copy(h, d, me).wait_send()
            mix_copy(h, d, source(d)).wait_recv()

    each_chip(chips_done)
    each_peer(peers_done)
    for copy in kept:
        copy.wait()
    last.wait()


PIECES = 4


def hand_over(a_in, b_in, a_out, b_out, room, sem):
    reads, writes = [], []
    for k, (src, dst) in enumerate(((a_in, a_out), (b_in, b_out))):
        for i in range(PIECES):
            piece = pl.ds(i * (ROWS // PIECES), ROWS // PIECES)
            reads.append(pltpu.make_async_copy(src.at[piece], room.at[k, piece], sem.at[0, k, i]))
            writes.append(pltpu.make_async_copy(room.at[k, piece], dst.at[piece], sem.at[1, k, i]))
    for copy in reads:
        copy.start()
    for read, write in zip(reads, writes):
        read.wait()
        write.start()
    for copy in writes:
        copy.wait()


def local(hyena_q, hyena_k, hyena_v, short_filter, residue, decay_rate, att_query, att_key, att_value):
    residue, decay_rate = residue.T, decay_rate.T
    vmem = pltpu.VMEM
    dma = pltpu.SemaphoreType.DMA
    hbm = pl.BlockSpec(memory_space=pltpu.HBM)
    result = jax.ShapeDtypeStruct((ROWS, D), bf16)
    hyena_out, att_out = pl.pallas_call(
        kernel,
        out_shape=(result, result),
        in_specs=[hbm] * 9,
        out_specs=(hbm, hbm),
        scratch_shapes=[
            vmem((3, ROWS, D), bf16),
            vmem(short_filter.shape, f32),
            vmem(residue.shape, f32),
            vmem(decay_rate.shape, f32),
            vmem((6 * D // 128, 128), f32),
            vmem((6 * D // 128, 128), bf16),
            vmem((6 * D // 128, 128), bf16),
            vmem((2 * STATE, 128), f32),
            vmem((N * 2 * STATE, 128), f32),
            vmem((STATE, 128), f32),
            vmem((CHIPS * STATE, 128), f32),
            vmem((ROWS, D), f32),
            vmem((ROWS * 32, 128), f32),
            vmem((ROWS * 32, 128), f32),
            vmem((3, ROWS + 8, 128), f32),
            vmem((N * STATE, 128), f32),
            vmem((CHIPS * STATE, 128), f32),
            vmem((CHIPS * STATE, 128), f32),
            vmem((CHIPS * STATE, 128), f32),
            vmem((CHIPS * STATE, 128), f32),
            vmem((CHIPS * STATE, 128), f32),
            vmem((CHIPS * STATE, 128), f32),
            vmem((N * STATE, 128), f32),
            vmem((HEADS, 3, SEQ, HEAD), bf16),
            vmem((HEADS, SEQ, HEAD), bf16),
            vmem((ROWS, D), bf16),
            pltpu.SemaphoreType.REGULAR,
            dma((6,)),
            dma((HEADS, 3)),
            dma((3,)),
            dma((4,)),
            dma((4,)),
            dma((CHIPS,)),
            dma((CHIPS,)),
            dma((CHIPS,)),
            dma((CHIPS,)),
            dma((CHIPS,)),
            dma((CHIPS,)),
            dma((HEADS, 3, N)),
            dma((HEADS, 3, N)),
            dma((HEADS, N)),
            dma((HEADS, N)),
        ],
        compiler_params=pltpu.CompilerParams(
            collective_id=0, has_side_effects=True, vmem_limit_bytes=63 * 2**20
        ),
    )(hyena_q, hyena_k, hyena_v, short_filter, residue, decay_rate, att_query, att_key, att_value)
    return pl.pallas_call(
        hand_over,
        out_shape=(result, result),
        in_specs=[hbm, hbm],
        out_specs=(hbm, hbm),
        scratch_shapes=[vmem((2, ROWS, D), bf16), dma((2, 2, PIECES))],
        compiler_params=pltpu.CompilerParams(vmem_limit_bytes=63 * 2**20),
    )(hyena_out, att_out)


def solution(mesh):
    rows = P(("dp", "ctx"), None)
    placed = (rows, rows, rows, P(), P("ctx", None), P("ctx", None), rows, rows, rows)
    return jax.shard_map(local, mesh=mesh, in_specs=placed, out_specs=(rows, rows), check_vma=False)
```

```python
import functools
import math

import jax
import jax.numpy as jnp
from jax import lax
from jax.experimental import pallas as pl
from jax.experimental.pallas import tpu as pltpu
from jax.sharding import PartitionSpec as P

MESH = pl.DeviceIdType.MESH
f32, bf16 = jnp.float32, jnp.bfloat16

N = 16
CHIPS = N // 2
NEAR = CHIPS + 2
ROWS = 128
SEQ = N * ROWS
D = 4096
MODES = 16
HEAD = 128
HEADS = D // HEAD // N
QBLOCK = 256
EXP2_SCALE = HEAD**-0.5 * math.log2(math.e)
STATE = MODES * 2


def row_of(j):
    return j % 2 * 16 + j // 2 % 2 * 8 + j // 4


def total(terms):
    while len(terms) > 1:
        terms = [a + b for a, b in zip(terms[::2], terms[1::2])]
    return terms[0]


def attend(q_ref, k_ref, v_ref, o_ref, block):
    end = (block + 1) * QBLOCK
    start = end - QBLOCK
    scores = lax.dot_general(
        q_ref[start:end, :], k_ref[:end, :], (((1,), (1,)), ((), ())), preferred_element_type=f32
    )
    row = lax.broadcasted_iota(jnp.int32, (QBLOCK, QBLOCK), 0)
    col = lax.broadcasted_iota(jnp.int32, (QBLOCK, QBLOCK), 1)
    diagonal = jnp.where(col <= row, scores[:, start:], -jnp.inf)
    top = jnp.max(diagonal, axis=1, keepdims=True)
    if block:
        top = jnp.maximum(top, jnp.max(scores[:, :start], axis=1, keepdims=True))
        scores = jnp.concatenate([scores[:, :start], diagonal], axis=1)
    else:
        scores = diagonal
    expo = jnp.exp2((scores - top) * EXP2_SCALE)
    denominator = jnp.sum(expo, axis=1, keepdims=True)
    mixed = jnp.dot(expo.astype(bf16), v_ref[:end, :], preferred_element_type=f32)
    o_ref[start:end, :] = (mixed / denominator).astype(bf16)


def edge_at(j, f, r):
    return pl.ds(j * 6 + 2 * f + r, 1)


def pack_edge(hx, wide):
    def column(j, carry):
        cs = pl.ds(pl.multiple_of(j * 128, 128), 128)
        for f in range(3):
            last = hx[f, ROWS - 16 : ROWS, cs].astype(f32)
            for r in range(2):
                wide[edge_at(j, f, r), :] = last[14 + r : 15 + r]
        return carry

    lax.fori_loop(0, D // 128, column, 0)


def short_filters(hx, halo, taps, qs, product, shifted):
    def column(j, carry):
        cs = pl.ds(pl.multiple_of(j * 128, 128), 128)

        def mix(f):
            x = hx[f, :, cs].astype(f32)
            shifted[f, 8 : 8 + ROWS, :] = x
            for r in range(2):
                shifted[f, 6 + r : 7 + r, :] = halo[edge_at(j, f, r), :]
            w = taps[f, :, cs]
            return (
                w[0:1] * x + w[1:2] * shifted[f, 7 : 7 + ROWS, :] + w[2:3] * shifted[f, 6 : 6 + ROWS, :]
            )

        qs[:, cs] = mix(0)
        both = (mix(1) * mix(2)).astype(bf16).astype(f32)
        product[pl.ds(row_of(j), ROWS, stride=32), :] = both
        return carry

    lax.fori_loop(0, D // 128, column, 0)


def mode_rows(ref, g, n, per_owner, first=0):
    return pl.ds(g % 2 * 8 * per_owner + first + n * 2 + g // 2, 8, stride=per_owner)


def scan(params, product, smooth, states):
    for g in range(4):
        power = [params[mode_rows(params, g, n, 2 * STATE), :] for n in range(MODES)]
        weight = [params[mode_rows(params, g, n, 2 * STATE, STATE), :] for n in range(MODES)]

        def step(t, state):
            rows = pl.ds(pl.multiple_of(t * 32 + g * 8, 8), 8)
            x = product[rows, :]
            state = [h * p + x for h, p in zip(state, power)]
            smooth[rows, :] = total([h * w for h, w in zip(state, weight)])
            return state

        state = lax.fori_loop(0, ROWS, step, [jnp.zeros((8, 128), f32)] * MODES, unroll=4)
        for n in range(MODES):
            states[mode_rows(states, g, n, STATE), :] = state[n]


def add_carried(params, carried, smooth):
    for g in range(4):
        power = [params[mode_rows(params, g, n, 2 * STATE), :] for n in range(MODES)]
        first = [
            params[mode_rows(params, g, n, 2 * STATE, STATE), :]
            * power[n]
            * carried[mode_rows(carried, g, n, STATE), :]
            for n in range(MODES)
        ]

        def step(t, term):
            rows = pl.ds(pl.multiple_of(t * 32 + g * 8, 8), 8)
            smooth[rows, :] = smooth[rows, :] + total(term)
            return [a * p for a, p in zip(term, power)]

        lax.fori_loop(0, ROWS, step, first, unroll=4)


def gate(smooth, qs, out):
    def column(j, carry):
        cs = pl.ds(pl.multiple_of(j * 128, 128), 128)
        y = smooth[pl.ds(row_of(j), ROWS, stride=32), :]
        out[:, cs] = (qs[:, cs] * y.astype(bf16).astype(f32)).astype(bf16)
        return carry

    lax.fori_loop(0, D // 128, column, 0, unroll=4)


def kernel(
    hq, hk, hv, taps_in, residue_in, decay_in, aq, ak, av,
    hyena_out, att_out,
    hx, taps, residue, decay, wide, edge, halo, mine, params, leap, step, qs, product, smooth, shifted,
    ends, pair, joint, gathered, chained, start, beside, carried, qkv, mixed, gated,
    ready, load_sem, out_sem, one_s, one_r,
    par_s, par_r, end_s, end_r, cha_s, cha_r, qkv_s, qkv_r, mix_s, mix_r,
):
    me = lax.axis_index("ctx")
    core = me % 2
    chip = me // 2
    other = me + 1 - 2 * core

    def target(d):
        z = (chip + d // 2) % 4
        return (me // 8 + d // 8) % 2 * 8 + z * 2 + (me + d) % 2

    def each_peer(do, last_first=False, begin=1, end=N):
        def at(d, carry):
            do(begin + end - 1 - d if last_first else d)
            return carry

        lax.fori_loop(begin, end, at, 0)

    def each_chip(do, begin=1, end=CHIPS):
        def at(e, carry):
            do(2 * e)
            return carry

        lax.fori_loop(begin, end, at, 0)

    def rows(p, count):
        return pl.ds(pl.multiple_of(p * count, count), count)

    def columns(p, h):
        return pl.ds(pl.multiple_of((p * HEADS + h) * HEAD, HEAD), HEAD)

    def remote(src, dst, send, recv, device):
        return pltpu.make_async_remote_copy(
            src_ref=src, dst_ref=dst, send_sem=send, recv_sem=recv,
            device_id={"ctx": device}, device_id_type=MESH,
        )

    loads = [
        pltpu.make_async_copy(src, dst, load_sem.at[min(i, 3)])
        for i, (src, dst) in enumerate(
            [(residue_in, residue), (decay_in, decay), (taps_in, taps)]
            + [(x, hx.at[f]) for f, x in enumerate((hq, hk, hv))]
        )
    ]

    def all_in(ref, sem):
        pltpu.make_async_copy(ref, ref, sem).wait()

    def all_out(ref, sem):
        remote(ref, ref, sem, sem, other).wait_send()


    barrier = pltpu.get_barrier_semaphore()
    each_peer(
        lambda d: pl.semaphore_signal(barrier, inc=1, device_id={"ctx": target(d)}, device_id_type=MESH),
        last_first=True,
        end=NEAR,
    )
    for copy in loads:
        copy.start()

    att = (aq, ak, av)
    for h in range(HEADS):
        for t in range(3):
            pltpu.make_async_copy(
                att[t].at[:, columns(me, h)], qkv.at[h, t, rows(me, ROWS)], qkv_r.at[h]
            ).start()

    loads[0].wait()
    loads[1].wait()
    rate = decay[...]
    weight = residue[...]
    for half in range(2):
        cs = slice(half * 128, half * 128 + 128)
        mine[pl.ds(half, MODES, stride=2), :] = jnp.exp(-rate[:, cs])
        mine[pl.ds(STATE + half, MODES, stride=2), :] = weight[:, cs]
        leap[pl.ds(half, MODES, stride=2), :] = jnp.exp(-(rate[:, cs] * float(2 * ROWS)))
    slot = core * CHIPS + chip
    params[rows(slot, 2 * STATE), :] = mine[...]
    loads[2].wait()
    all_in(hx, load_sem.at[3])
    pack_edge(hx, wide)
    edge[...] = wide[...].astype(bf16)

    pl.semaphore_wait(barrier, NEAR - 1)
    pl.semaphore_signal(ready, inc=1, device_id={"ctx": target(N // 2)}, device_id_type=MESH)

    halo_copy = remote(edge, halo, one_s.at[0], one_r.at[0], (me + 1) % N)
    half_rows = CHIPS * 2 * STATE
    par_on = remote(
        params.at[rows(core, half_rows)], params.at[rows(core, half_rows)], one_s.at[1], one_r.at[1], other
    )
    end_on = remote(ends.at[rows(1 - core, CHIPS * STATE)], pair, one_s.at[2], one_r.at[2], other)
    cha_on = remote(beside, carried.at[rows(core, CHIPS * STATE)], one_s.at[3], one_r.at[3], other)

    def par_copy(d, p):
        return remote(
            mine, params.at[rows(core * CHIPS + p // 2, 2 * STATE)], par_s, par_r, target(d)
        )

    def end_copy(d, p):
        return remote(
            joint.at[rows(target(d) // 2, STATE)], gathered.at[rows(p // 2, STATE)],
            end_s, end_r, target(d),
        )

    def cha_copy(d, p):
        return remote(
            chained.at[rows(target(d) // 2, STATE)], start.at[rows(p // 2, STATE)],
            cha_s, cha_r, target(d),
        )

    def qkv_copy(h, t, d, p):
        return remote(
            att[t].at[:, columns(target(d), h)], qkv.at[h, t, rows(p, ROWS)],
            qkv_s, qkv_r.at[h], target(d),
        )

    def mix_copy(h, d, p):
        return remote(
            mixed.at[h, rows(target(d), ROWS)], att_out.at[:, columns(p, h)],
            mix_s, mix_r, target(d),
        )

    def qkv_start(h, tensors, begin=1, end=N):
        def one(d):
            for t in tensors:
                qkv_copy(h, t, d, me).start()

        each_peer(one, last_first=True, begin=begin, end=end)

    each_chip(lambda d: par_copy(d, me).start(), 1, CHIPS // 2 + 1)
    qkv_start(0, (0,), end=NEAR)
    pl.semaphore_wait(ready, 1)
    each_chip(lambda d: par_copy(d, me).start(), CHIPS // 2 + 1, CHIPS)

    @pl.when(me < N - 1)
    def _():
        halo_copy.start()

    qkv_start(0, (0,), begin=NEAR)
    qkv_start(0, (1, 2))

    @pl.when(me > 0)
    def _():
        halo_copy.wait_recv()
        wide[...] = halo[...].astype(f32)

    @pl.when(me == 0)
    def _():
        wide[...] = jnp.zeros_like(wide)

    short_filters(hx, wide, taps, qs, product, shifted)
    all_in(params.at[pl.ds(0, (CHIPS - 1) * 2 * STATE)], par_r)
    par_on.start()
    par_on.wait_recv()
    scan(params, product, smooth, ends)
    end_on.start()

    for p in range(CHIPS):
        power = params[pl.ds(pl.multiple_of(core * half_rows + p * 2 * STATE, STATE), STATE), :]
        for _ in range(7):
            power = power * power
        step[p * STATE : (p + 1) * STATE, :] = power

    end_on.wait_recv()
    same = ends[rows(core, CHIPS * STATE), :]
    first = jnp.where(core == 0, same, pair[...])
    joint[...] = first * step[...] + jnp.where(core == 0, pair[...], same)
    gathered[rows(chip, STATE), :] = joint[rows(chip, STATE), :]
    each_chip(lambda d: end_copy(d, me).start())
    qkv_start(1, (0, 1, 2))

    def attention(h):
        all_in(qkv.at[h], qkv_r.at[h])
        for block in range(SEQ // QBLOCK):
            attend(qkv.at[h, 0], qkv.at[h, 1], qkv.at[h, 2], mixed.at[h], block)

    def mix_start(h):
        each_peer(lambda d: mix_copy(h, d, me).start(), last_first=True)
        pltpu.make_async_copy(mixed.at[h, rows(me, ROWS)], att_out.at[:, columns(me, h)], mix_r).start()

    attention(0)

    all_in(gathered.at[pl.ds(0, (CHIPS - 1) * STATE)], end_r)

    def chain(p, state):
        chained[rows(p, STATE), :] = state
        return state * leap[...] + gathered[rows(p, STATE), :]

    lax.fori_loop(0, CHIPS, chain, jnp.zeros((STATE, 128), f32))
    start[rows(chip, STATE), :] = chained[rows(chip, STATE), :]
    each_chip(lambda d: cha_copy(d, me).start())

    mix_start(0)

    attention(1)
    mix_start(1)

    all_in(start.at[pl.ds(0, (CHIPS - 1) * STATE)], cha_r)
    same = ends[rows(core, CHIPS * STATE), :]
    first = jnp.where(core == 0, same, pair[...])
    even = start[...]
    odd = even * step[...] + first
    carried[rows(core, CHIPS * STATE), :] = jnp.where(core == 0, even, odd)
    beside[...] = jnp.where(core == 0, odd, even)
    cha_on.start()
    cha_on.wait_recv()
    add_carried(params, carried, smooth)
    gate(smooth, qs, gated)
    last = pltpu.make_async_copy(gated, hyena_out, out_sem)
    last.start()

    @pl.when(me < N - 1)
    def _():
        halo_copy.wait_send()

    for copy in (par_on, end_on, cha_on):
        copy.wait_send()

    all_out(params.at[pl.ds(0, (CHIPS - 1) * 2 * STATE)], par_s)
    all_out(joint.at[pl.ds(0, (CHIPS - 1) * STATE)], end_s)
    all_out(chained.at[pl.ds(0, (CHIPS - 1) * STATE)], cha_s)
    all_out(qkv.at[:, :, pl.ds(0, (N - 1) * ROWS)], qkv_s)
    all_out(mixed.at[:, pl.ds(0, (N - 1) * ROWS)], mix_s)
    all_in(att_out, mix_r)
    last.wait()


PIECES = 4


def hand_over(a_in, b_in, a_out, b_out, room, sem):
    reads, writes = [], []
    for k, (src, dst) in enumerate(((a_in, a_out), (b_in, b_out))):
        for i in range(PIECES):
            piece = pl.ds(i * (ROWS // PIECES), ROWS // PIECES)
            reads.append(pltpu.make_async_copy(src.at[piece], room.at[k, piece], sem.at[0, k, i]))
            writes.append(pltpu.make_async_copy(room.at[k, piece], dst.at[piece], sem.at[1, k, i]))
    for copy in reads:
        copy.start()
    for read, write in zip(reads, writes):
        read.wait()
        write.start()
    for copy in writes:
        copy.wait()


def local(hyena_q, hyena_k, hyena_v, short_filter, residue, decay_rate, att_query, att_key, att_value):
    residue, decay_rate = residue.T, decay_rate.T
    vmem = pltpu.VMEM
    dma = pltpu.SemaphoreType.DMA
    hbm = pl.BlockSpec(memory_space=pltpu.HBM)
    result = jax.ShapeDtypeStruct((ROWS, D), bf16)
    hyena_out, att_out = pl.pallas_call(
        kernel,
        out_shape=(result, result),
        in_specs=[hbm] * 9,
        out_specs=(hbm, hbm),
        scratch_shapes=[
            vmem((3, ROWS, D), bf16),
            vmem(short_filter.shape, f32),
            vmem(residue.shape, f32),
            vmem(decay_rate.shape, f32),
            vmem((6 * D // 128, 128), f32),
            vmem((6 * D // 128, 128), bf16),
            vmem((6 * D // 128, 128), bf16),
            vmem((2 * STATE, 128), f32),
            vmem((N * 2 * STATE, 128), f32),
            vmem((STATE, 128), f32),
            vmem((CHIPS * STATE, 128), f32),
            vmem((ROWS, D), f32),
            vmem((ROWS * 32, 128), f32),
            vmem((ROWS * 32, 128), f32),
            vmem((3, ROWS + 8, 128), f32),
            vmem((N * STATE, 128), f32),
            vmem((CHIPS * STATE, 128), f32),
            vmem((CHIPS * STATE, 128), f32),
            vmem((CHIPS * STATE, 128), f32),
            vmem((CHIPS * STATE, 128), f32),
            vmem((CHIPS * STATE, 128), f32),
            vmem((CHIPS * STATE, 128), f32),
            vmem((N * STATE, 128), f32),
            vmem((HEADS, 3, SEQ, HEAD), bf16),
            vmem((HEADS, SEQ, HEAD), bf16),
            vmem((ROWS, D), bf16),
            pltpu.SemaphoreType.REGULAR,
            dma((4,)),
            dma,
            dma((4,)),
            dma((4,)),
            dma,
            dma,
            dma,
            dma,
            dma,
            dma,
            dma,
            dma((HEADS,)),
            dma,
            dma,
        ],
        compiler_params=pltpu.CompilerParams(
            collective_id=0, has_side_effects=True, vmem_limit_bytes=63 * 2**20
        ),
    )(hyena_q, hyena_k, hyena_v, short_filter, residue, decay_rate, att_query, att_key, att_value)
    return pl.pallas_call(
        hand_over,
        out_shape=(result, result),
        in_specs=[hbm, hbm],
        out_specs=(hbm, hbm),
        scratch_shapes=[vmem((2, ROWS, D), bf16), dma((2, 2, PIECES))],
        compiler_params=pltpu.CompilerParams(vmem_limit_bytes=63 * 2**20),
    )(hyena_out, att_out)


def solution(mesh):
    rows = P(("dp", "ctx"), None)
    placed = (rows, rows, rows, P(), P("ctx", None), P("ctx", None), rows, rows, rows)
    return jax.shard_map(local, mesh=mesh, in_specs=placed, out_specs=(rows, rows), check_vma=False)
```

```python
import functools
import math

import jax
import jax.numpy as jnp
from jax import lax
from jax.experimental import pallas as pl
from jax.experimental.pallas import tpu as pltpu
from jax.sharding import PartitionSpec as P

MESH = pl.DeviceIdType.MESH
f32, bf16 = jnp.float32, jnp.bfloat16

N = 16
CHIPS = N // 2
NEAR = CHIPS + 2
ROWS = 128
SEQ = N * ROWS
D = 4096
MODES = 16
HEAD = 128
HEADS = D // HEAD // N
QBLOCK = 256
EXP2_SCALE = HEAD**-0.5 * math.log2(math.e)
STATE = MODES * 2


def row_of(j):
    return j % 2 * 16 + j // 2 % 2 * 8 + j // 4


def total(terms):
    while len(terms) > 1:
        terms = [a + b for a, b in zip(terms[::2], terms[1::2])]
    return terms[0]


def weigh(q_ref, k_ref, weights, sums, block):
    end = (block + 1) * QBLOCK
    start = end - QBLOCK
    scores = lax.dot_general(
        q_ref[start:end, :], k_ref[:end, :], (((1,), (1,)), ((), ())), preferred_element_type=f32
    )
    row = lax.broadcasted_iota(jnp.int32, (QBLOCK, QBLOCK), 0)
    col = lax.broadcasted_iota(jnp.int32, (QBLOCK, QBLOCK), 1)
    diagonal = jnp.where(col <= row, scores[:, start:], -jnp.inf)
    top = jnp.max(diagonal, axis=1, keepdims=True)
    if block:
        top = jnp.maximum(top, jnp.max(scores[:, :start], axis=1, keepdims=True))
        scores = jnp.concatenate([scores[:, :start], diagonal], axis=1)
    else:
        scores = diagonal
    expo = jnp.exp2((scores - top) * EXP2_SCALE)
    sums[start:end, :] = jnp.broadcast_to(jnp.sum(expo, axis=1, keepdims=True), (QBLOCK, HEAD))
    weights[start:end, :end] = expo.astype(bf16)


def blend(weights, sums, v_ref, o_ref, block):
    end = (block + 1) * QBLOCK
    start = end - QBLOCK
    mixed = jnp.dot(weights[start:end, :end], v_ref[:end, :], preferred_element_type=f32)
    o_ref[start:end, :] = (mixed / sums[start:end, :]).astype(bf16)


def edge_at(j, f, r):
    return pl.ds(j * 6 + 2 * f + r, 1)


def pack_edge(hx, wide):
    def column(j, carry):
        cs = pl.ds(pl.multiple_of(j * 128, 128), 128)
        for f in range(3):
            last = hx[f, ROWS - 16 : ROWS, cs].astype(f32)
            for r in range(2):
                wide[edge_at(j, f, r), :] = last[14 + r : 15 + r]
        return carry

    lax.fori_loop(0, D // 128, column, 0)


def short_filters(hx, halo, taps, qs, product, shifted):
    def column(j, carry):
        cs = pl.ds(pl.multiple_of(j * 128, 128), 128)

        def mix(f):
            x = hx[f, :, cs].astype(f32)
            shifted[f, 8 : 8 + ROWS, :] = x
            for r in range(2):
                shifted[f, 6 + r : 7 + r, :] = halo[edge_at(j, f, r), :]
            w = taps[f, :, cs]
            return (
                w[0:1] * x + w[1:2] * shifted[f, 7 : 7 + ROWS, :] + w[2:3] * shifted[f, 6 : 6 + ROWS, :]
            )

        qs[:, cs] = mix(0)
        both = (mix(1) * mix(2)).astype(bf16).astype(f32)
        product[pl.ds(row_of(j), ROWS, stride=32), :] = both
        return carry

    lax.fori_loop(0, D // 128, column, 0)


def mode_rows(ref, g, n, per_owner, first=0):
    return pl.ds(g % 2 * 8 * per_owner + first + n * 2 + g // 2, 8, stride=per_owner)


def scan(params, product, smooth, states):
    for g in range(4):
        power = [params[mode_rows(params, g, n, 2 * STATE), :] for n in range(MODES)]
        weight = [params[mode_rows(params, g, n, 2 * STATE, STATE), :] for n in range(MODES)]

        def step(t, state):
            rows = pl.ds(pl.multiple_of(t * 32 + g * 8, 8), 8)
            x = product[rows, :]
            state = [h * p + x for h, p in zip(state, power)]
            smooth[rows, :] = total([h * w for h, w in zip(state, weight)])
            return state

        state = lax.fori_loop(0, ROWS, step, [jnp.zeros((8, 128), f32)] * MODES, unroll=4)
        for n in range(MODES):
            states[mode_rows(states, g, n, STATE), :] = state[n]


def add_carried(params, carried, smooth):
    for g in range(4):
        power = [params[mode_rows(params, g, n, 2 * STATE), :] for n in range(MODES)]
        first = [
            params[mode_rows(params, g, n, 2 * STATE, STATE), :]
            * power[n]
            * carried[mode_rows(carried, g, n, STATE), :]
            for n in range(MODES)
        ]

        def step(t, term):
            rows = pl.ds(pl.multiple_of(t * 32 + g * 8, 8), 8)
            smooth[rows, :] = smooth[rows, :] + total(term)
            return [a * p for a, p in zip(term, power)]

        lax.fori_loop(0, ROWS, step, first, unroll=4)


def gate(smooth, qs, out):
    def column(j, carry):
        cs = pl.ds(pl.multiple_of(j * 128, 128), 128)
        y = smooth[pl.ds(row_of(j), ROWS, stride=32), :]
        out[:, cs] = (qs[:, cs] * y.astype(bf16).astype(f32)).astype(bf16)
        return carry

    lax.fori_loop(0, D // 128, column, 0, unroll=4)


def kernel(
    hq, hk, hv, taps_in, residue_in, decay_in, aq, ak, av,
    hyena_out, att_out,
    hx, taps, residue, decay, wide, edge, halo, mine, params, leap, step, qs, product, smooth, shifted,
    ends, pair, joint, gathered, chained, start, beside, carried, qkv, weights, sums, mixed, gated,
    ready, load_sem, out_sem, one_s, one_r,
    par_s, par_r, end_s, end_r, cha_s, cha_r, qkv_s, qkv_r, mix_s, mix_r,
):
    me = lax.axis_index("ctx")
    core = me % 2
    chip = me // 2
    other = me + 1 - 2 * core

    def target(d):
        z = (chip + d // 2) % 4
        return (me // 8 + d // 8) % 2 * 8 + z * 2 + (me + d) % 2

    def each_peer(do, last_first=False, begin=1, end=N):
        def at(d, carry):
            do(begin + end - 1 - d if last_first else d)
            return carry

        lax.fori_loop(begin, end, at, 0)

    def each_chip(do, begin=1, end=CHIPS):
        def at(e, carry):
            do(2 * e)
            return carry

        lax.fori_loop(begin, end, at, 0)

    def rows(p, count):
        return pl.ds(pl.multiple_of(p * count, count), count)

    def columns(p, h):
        return pl.ds(pl.multiple_of((p * HEADS + h) * HEAD, HEAD), HEAD)

    def remote(src, dst, send, recv, device):
        return pltpu.make_async_remote_copy(
            src_ref=src, dst_ref=dst, send_sem=send, recv_sem=recv,
            device_id={"ctx": device}, device_id_type=MESH,
        )

    loads = [
        pltpu.make_async_copy(src, dst, load_sem.at[min(i, 3)])
        for i, (src, dst) in enumerate(
            [(residue_in, residue), (decay_in, decay), (taps_in, taps)]
            + [(x, hx.at[f]) for f, x in enumerate((hq, hk, hv))]
        )
    ]

    def all_in(ref, sem):
        pltpu.make_async_copy(ref, ref, sem).wait()

    def all_out(ref, sem):
        remote(ref, ref, sem, sem, other).wait_send()


    barrier = pltpu.get_barrier_semaphore()
    each_peer(
        lambda d: pl.semaphore_signal(barrier, inc=1, device_id={"ctx": target(d)}, device_id_type=MESH),
        last_first=True,
        end=NEAR,
    )
    for copy in loads:
        copy.start()

    att = (aq, ak, av)
    for h in range(HEADS):
        for t in range(3):
            pltpu.make_async_copy(
                att[t].at[:, columns(me, h)], qkv.at[h, t, rows(me, ROWS)], qkv_r.at[h, t // 2]
            ).start()

    loads[0].wait()
    loads[1].wait()
    rate = decay[...]
    weight = residue[...]
    for half in range(2):
        cs = slice(half * 128, half * 128 + 128)
        mine[pl.ds(half, MODES, stride=2), :] = jnp.exp(-rate[:, cs])
        mine[pl.ds(STATE + half, MODES, stride=2), :] = weight[:, cs]
        leap[pl.ds(half, MODES, stride=2), :] = jnp.exp(-(rate[:, cs] * float(2 * ROWS)))
    slot = core * CHIPS + chip
    params[rows(slot, 2 * STATE), :] = mine[...]
    loads[2].wait()
    all_in(hx, load_sem.at[3])
    pack_edge(hx, wide)
    edge[...] = wide[...].astype(bf16)

    pl.semaphore_wait(barrier, NEAR - 1)
    pl.semaphore_signal(ready, inc=1, device_id={"ctx": target(N // 2)}, device_id_type=MESH)

    halo_copy = remote(edge, halo, one_s.at[0], one_r.at[0], (me + 1) % N)
    half_rows = CHIPS * 2 * STATE
    par_on = remote(
        params.at[rows(core, half_rows)], params.at[rows(core, half_rows)], one_s.at[1], one_r.at[1], other
    )
    end_on = remote(ends.at[rows(1 - core, CHIPS * STATE)], pair, one_s.at[2], one_r.at[2], other)
    cha_on = remote(beside, carried.at[rows(core, CHIPS * STATE)], one_s.at[3], one_r.at[3], other)

    def par_copy(d, p):
        return remote(
            mine, params.at[rows(core * CHIPS + p // 2, 2 * STATE)], par_s, par_r, target(d)
        )

    def end_copy(d, p):
        return remote(
            joint.at[rows(target(d) // 2, STATE)], gathered.at[rows(p // 2, STATE)],
            end_s, end_r, target(d),
        )

    def cha_copy(d, p):
        return remote(
            chained.at[rows(target(d) // 2, STATE)], start.at[rows(p // 2, STATE)],
            cha_s, cha_r, target(d),
        )

    def qkv_copy(h, t, d, p):
        return remote(
            att[t].at[:, columns(target(d), h)], qkv.at[h, t, rows(p, ROWS)],
            qkv_s, qkv_r.at[h, t // 2], target(d),
        )

    def mix_copy(h, d, p):
        return remote(
            mixed.at[h, rows(target(d), ROWS)], att_out.at[:, columns(p, h)],
            mix_s, mix_r, target(d),
        )

    def qkv_start(h, tensors, begin=1, end=N):
        def one(d):
            for t in tensors:
                qkv_copy(h, t, d, me).start()

        each_peer(one, last_first=True, begin=begin, end=end)

    each_chip(lambda d: par_copy(d, me).start(), 1, CHIPS // 2 + 1)
    qkv_start(0, (0,), end=NEAR)
    pl.semaphore_wait(ready, 1)
    each_chip(lambda d: par_copy(d, me).start(), CHIPS // 2 + 1, CHIPS)

    @pl.when(me < N - 1)
    def _():
        halo_copy.start()

    qkv_start(0, (0,), begin=NEAR)
    qkv_start(0, (1, 2))
    qkv_start(1, (0,))

    @pl.when(me > 0)
    def _():
        halo_copy.wait_recv()
        wide[...] = halo[...].astype(f32)

    @pl.when(me == 0)
    def _():
        wide[...] = jnp.zeros_like(wide)

    short_filters(hx, wide, taps, qs, product, shifted)
    all_in(params.at[pl.ds(0, (CHIPS - 1) * 2 * STATE)], par_r)
    par_on.start()
    par_on.wait_recv()
    scan(params, product, smooth, ends)
    end_on.start()

    for p in range(CHIPS):
        power = params[pl.ds(pl.multiple_of(core * half_rows + p * 2 * STATE, STATE), STATE), :]
        for _ in range(7):
            power = power * power
        step[p * STATE : (p + 1) * STATE, :] = power

    end_on.wait_recv()
    same = ends[rows(core, CHIPS * STATE), :]
    first = jnp.where(core == 0, same, pair[...])
    joint[...] = first * step[...] + jnp.where(core == 0, pair[...], same)
    gathered[rows(chip, STATE), :] = joint[rows(chip, STATE), :]
    each_chip(lambda d: end_copy(d, me).start())
    qkv_start(1, (1,))
    qkv_start(1, (2,))

    def attention(h):
        all_in(qkv.at[h, pl.ds(0, 2)], qkv_r.at[h, 0])
        for block in range(SEQ // QBLOCK):
            weigh(qkv.at[h, 0], qkv.at[h, 1], weights, sums, block)
        all_in(qkv.at[h, 2], qkv_r.at[h, 1])
        for block in range(SEQ // QBLOCK):
            blend(weights, sums, qkv.at[h, 2], mixed.at[h], block)

    def mix_start(h):
        each_peer(lambda d: mix_copy(h, d, me).start(), last_first=True)
        pltpu.make_async_copy(mixed.at[h, rows(me, ROWS)], att_out.at[:, columns(me, h)], mix_r).start()

    attention(0)

    all_in(gathered.at[pl.ds(0, (CHIPS - 1) * STATE)], end_r)

    def chain(p, state):
        chained[rows(p, STATE), :] = state
        return state * leap[...] + gathered[rows(p, STATE), :]

    lax.fori_loop(0, CHIPS, chain, jnp.zeros((STATE, 128), f32))
    start[rows(chip, STATE), :] = chained[rows(chip, STATE), :]
    each_chip(lambda d: cha_copy(d, me).start())

    mix_start(0)

    attention(1)
    mix_start(1)

    all_in(start.at[pl.ds(0, (CHIPS - 1) * STATE)], cha_r)
    same = ends[rows(core, CHIPS * STATE), :]
    first = jnp.where(core == 0, same, pair[...])
    even = start[...]
    odd = even * step[...] + first
    carried[rows(core, CHIPS * STATE), :] = jnp.where(core == 0, even, odd)
    beside[...] = jnp.where(core == 0, odd, even)
    cha_on.start()
    cha_on.wait_recv()
    add_carried(params, carried, smooth)
    gate(smooth, qs, gated)
    last = pltpu.make_async_copy(gated, hyena_out, out_sem)
    last.start()

    @pl.when(me < N - 1)
    def _():
        halo_copy.wait_send()

    for copy in (par_on, end_on, cha_on):
        copy.wait_send()

    all_out(params.at[pl.ds(0, (CHIPS - 1) * 2 * STATE)], par_s)
    all_out(joint.at[pl.ds(0, (CHIPS - 1) * STATE)], end_s)
    all_out(chained.at[pl.ds(0, (CHIPS - 1) * STATE)], cha_s)
    all_out(qkv.at[:, :, pl.ds(0, (N - 1) * ROWS)], qkv_s)
    all_out(mixed.at[:, pl.ds(0, (N - 1) * ROWS)], mix_s)
    all_in(att_out, mix_r)
    last.wait()


PIECES = 4


def hand_over(a_in, b_in, a_out, b_out, room, sem):
    reads, writes = [], []
    for k, (src, dst) in enumerate(((a_in, a_out), (b_in, b_out))):
        for i in range(PIECES):
            piece = pl.ds(i * (ROWS // PIECES), ROWS // PIECES)
            reads.append(pltpu.make_async_copy(src.at[piece], room.at[k, piece], sem.at[0, k, i]))
            writes.append(pltpu.make_async_copy(room.at[k, piece], dst.at[piece], sem.at[1, k, i]))
    for copy in reads:
        copy.start()
    for read, write in zip(reads, writes):
        read.wait()
        write.start()
    for copy in writes:
        copy.wait()


def local(hyena_q, hyena_k, hyena_v, short_filter, residue, decay_rate, att_query, att_key, att_value):
    residue, decay_rate = residue.T, decay_rate.T
    vmem = pltpu.VMEM
    dma = pltpu.SemaphoreType.DMA
    hbm = pl.BlockSpec(memory_space=pltpu.HBM)
    result = jax.ShapeDtypeStruct((ROWS, D), bf16)
    hyena_out, att_out = pl.pallas_call(
        kernel,
        out_shape=(result, result),
        in_specs=[hbm] * 9,
        out_specs=(hbm, hbm),
        scratch_shapes=[
            vmem((3, ROWS, D), bf16),
            vmem(short_filter.shape, f32),
            vmem(residue.shape, f32),
            vmem(decay_rate.shape, f32),
            vmem((6 * D // 128, 128), f32),
            vmem((6 * D // 128, 128), bf16),
            vmem((6 * D // 128, 128), bf16),
            vmem((2 * STATE, 128), f32),
            vmem((N * 2 * STATE, 128), f32),
            vmem((STATE, 128), f32),
            vmem((CHIPS * STATE, 128), f32),
            vmem((ROWS, D), f32),
            vmem((ROWS * 32, 128), f32),
            vmem((ROWS * 32, 128), f32),
            vmem((3, ROWS + 8, 128), f32),
            vmem((N * STATE, 128), f32),
            vmem((CHIPS * STATE, 128), f32),
            vmem((CHIPS * STATE, 128), f32),
            vmem((CHIPS * STATE, 128), f32),
            vmem((CHIPS * STATE, 128), f32),
            vmem((CHIPS * STATE, 128), f32),
            vmem((CHIPS * STATE, 128), f32),
            vmem((N * STATE, 128), f32),
            vmem((HEADS, 3, SEQ, HEAD), bf16),
            vmem((SEQ, SEQ), bf16),
            vmem((SEQ, HEAD), f32),
            vmem((HEADS, SEQ, HEAD), bf16),
            vmem((ROWS, D), bf16),
            pltpu.SemaphoreType.REGULAR,
            dma((4,)),
            dma,
            dma((4,)),
            dma((4,)),
            dma,
            dma,
            dma,
            dma,
            dma,
            dma,
            dma,
            dma((HEADS, 2)),
            dma,
            dma,
        ],
        compiler_params=pltpu.CompilerParams(
            collective_id=0, has_side_effects=True, vmem_limit_bytes=63 * 2**20
        ),
    )(hyena_q, hyena_k, hyena_v, short_filter, residue, decay_rate, att_query, att_key, att_value)
    return pl.pallas_call(
        hand_over,
        out_shape=(result, result),
        in_specs=[hbm, hbm],
        out_specs=(hbm, hbm),
        scratch_shapes=[vmem((2, ROWS, D), bf16), dma((2, 2, PIECES))],
        compiler_params=pltpu.CompilerParams(vmem_limit_bytes=63 * 2**20),
    )(hyena_out, att_out)


def solution(mesh):
    rows = P(("dp", "ctx"), None)
    placed = (rows, rows, rows, P(), P("ctx", None), P("ctx", None), rows, rows, rows)
    return jax.shard_map(local, mesh=mesh, in_specs=placed, out_specs=(rows, rows), check_vma=False)
```

```python
import functools
import math

import jax
import jax.numpy as jnp
from jax import lax
from jax.experimental import pallas as pl
from jax.experimental.pallas import tpu as pltpu
from jax.sharding import PartitionSpec as P

MESH = pl.DeviceIdType.MESH
f32, bf16 = jnp.float32, jnp.bfloat16

N = 16
CHIPS = N // 2
NEAR = CHIPS + 2
ROWS = 128
SEQ = N * ROWS
D = 4096
MODES = 16
HEAD = 128
HEADS = D // HEAD // N
QBLOCK = 256
EXP2_SCALE = HEAD**-0.5 * math.log2(math.e)
EDGE = 6 * D // 128
STATE = MODES * 2


def row_of(j):
    return j % 2 * 16 + j // 2 % 2 * 8 + j // 4


def total(terms):
    while len(terms) > 1:
        terms = [a + b for a, b in zip(terms[::2], terms[1::2])]
    return terms[0]


def weigh(q_ref, k_ref, weights, sums, block):
    end = (block + 1) * QBLOCK
    start = end - QBLOCK
    scores = lax.dot_general(
        q_ref[start:end, :], k_ref[:end, :], (((1,), (1,)), ((), ())), preferred_element_type=f32
    )
    row = lax.broadcasted_iota(jnp.int32, (QBLOCK, QBLOCK), 0)
    col = lax.broadcasted_iota(jnp.int32, (QBLOCK, QBLOCK), 1)
    diagonal = jnp.where(col <= row, scores[:, start:], -jnp.inf)
    top = jnp.max(diagonal, axis=1, keepdims=True)
    if block:
        top = jnp.maximum(top, jnp.max(scores[:, :start], axis=1, keepdims=True))
        scores = jnp.concatenate([scores[:, :start], diagonal], axis=1)
    else:
        scores = diagonal
    expo = jnp.exp2((scores - top) * EXP2_SCALE)
    sums[start:end, :] = jnp.broadcast_to(jnp.sum(expo, axis=1, keepdims=True), (QBLOCK, HEAD))
    weights[start:end, :end] = expo.astype(bf16)


def blend(weights, sums, v_ref, o_ref, block):
    end = (block + 1) * QBLOCK
    start = end - QBLOCK
    mixed = jnp.dot(weights[start:end, :end], v_ref[:end, :], preferred_element_type=f32)
    o_ref[start:end, :] = (mixed / sums[start:end, :]).astype(bf16)


def edge_at(j, f, r):
    return pl.ds(j * 6 + 2 * f + r, 1)


def pack_edge(hx, wide):
    def column(j, carry):
        cs = pl.ds(pl.multiple_of(j * 128, 128), 128)
        for f in range(3):
            last = hx[f, ROWS - 16 : ROWS, cs].astype(f32)
            for r in range(2):
                wide[edge_at(j, f, r), :] = last[14 + r : 15 + r]
        return carry

    lax.fori_loop(0, D // 128, column, 0)


def short_filters(hx, halo, taps, qs, product, shifted):
    def column(j, carry):
        cs = pl.ds(pl.multiple_of(j * 128, 128), 128)

        def mix(f):
            x = hx[f, :, cs].astype(f32)
            shifted[f, 8 : 8 + ROWS, :] = x
            for r in range(2):
                shifted[f, 6 + r : 7 + r, :] = halo[edge_at(j, f, r), :]
            w = taps[f, :, cs]
            return (
                w[0:1] * x + w[1:2] * shifted[f, 7 : 7 + ROWS, :] + w[2:3] * shifted[f, 6 : 6 + ROWS, :]
            )

        qs[:, cs] = mix(0)
        both = (mix(1) * mix(2)).astype(bf16).astype(f32)
        product[pl.ds(row_of(j), ROWS, stride=32), :] = both
        return carry

    lax.fori_loop(0, D // 128, column, 0)


def mode_rows(ref, g, n, per_owner, first=0):
    return pl.ds(g % 2 * 8 * per_owner + first + n * 2 + g // 2, 8, stride=per_owner)


def scan(params, product, smooth, states):
    for g in range(4):
        power = [params[mode_rows(params, g, n, 2 * STATE), :] for n in range(MODES)]
        weight = [params[mode_rows(params, g, n, 2 * STATE, STATE), :] for n in range(MODES)]

        def step(t, state):
            rows = pl.ds(pl.multiple_of(t * 32 + g * 8, 8), 8)
            x = product[rows, :]
            state = [h * p + x for h, p in zip(state, power)]
            smooth[rows, :] = total([h * w for h, w in zip(state, weight)])
            return state

        state = lax.fori_loop(0, ROWS, step, [jnp.zeros((8, 128), f32)] * MODES, unroll=4)
        for n in range(MODES):
            states[mode_rows(states, g, n, STATE), :] = state[n]


def add_carried(params, carried, smooth):
    for g in range(4):
        power = [params[mode_rows(params, g, n, 2 * STATE), :] for n in range(MODES)]
        first = [
            params[mode_rows(params, g, n, 2 * STATE, STATE), :]
            * power[n]
            * carried[mode_rows(carried, g, n, STATE), :]
            for n in range(MODES)
        ]

        def step(t, term):
            rows = pl.ds(pl.multiple_of(t * 32 + g * 8, 8), 8)
            smooth[rows, :] = smooth[rows, :] + total(term)
            return [a * p for a, p in zip(term, power)]

        lax.fori_loop(0, ROWS, step, first, unroll=4)


def gate(smooth, qs, out):
    def column(j, carry):
        cs = pl.ds(pl.multiple_of(j * 128, 128), 128)
        y = smooth[pl.ds(row_of(j), ROWS, stride=32), :]
        out[:, cs] = (qs[:, cs] * y.astype(bf16).astype(f32)).astype(bf16)
        return carry

    lax.fori_loop(0, D // 128, column, 0, unroll=4)


def kernel(
    hq, hk, hv, taps_in, residue_in, decay_in, aq, ak, av,
    hyena_out, att_out,
    hx, taps, residue, decay, wide, edge, halo, mine, params, leap, step, qs, product, smooth, shifted,
    ends, pair, joint, gathered, chained, start, beside, carried, qkv, weights, sums, mixed, gated,
    ready, load_sem, out_sem, one_s, one_r,
    par_s, par_r, end_s, end_r, cha_s, cha_r, qkv_s, qkv_r, mix_s, mix_r,
):
    me = lax.axis_index("ctx")
    core = me % 2
    chip = me // 2
    other = me + 1 - 2 * core

    def target(d):
        z = (chip + d // 2) % 4
        return (me // 8 + d // 8) % 2 * 8 + z * 2 + (me + d) % 2

    def each_peer(do, last_first=False, begin=1, end=N):
        def at(d, carry):
            do(begin + end - 1 - d if last_first else d)
            return carry

        lax.fori_loop(begin, end, at, 0)

    def each_chip(do, begin=1, end=CHIPS):
        def at(e, carry):
            do(2 * e)
            return carry

        lax.fori_loop(begin, end, at, 0)

    def rows(p, count):
        return pl.ds(pl.multiple_of(p * count, count), count)

    def columns(p, h):
        return pl.ds(pl.multiple_of((p * HEADS + h) * HEAD, HEAD), HEAD)

    def remote(src, dst, send, recv, device):
        return pltpu.make_async_remote_copy(
            src_ref=src, dst_ref=dst, send_sem=send, recv_sem=recv,
            device_id={"ctx": device}, device_id_type=MESH,
        )

    loads = [
        pltpu.make_async_copy(src, dst, load_sem.at[min(i, 3)])
        for i, (src, dst) in enumerate(
            [(residue_in, residue), (decay_in, decay), (taps_in, taps)]
            + [(x, hx.at[f]) for f, x in enumerate((hq, hk, hv))]
        )
    ]

    def all_in(ref, sem):
        pltpu.make_async_copy(ref, ref, sem).wait()

    def all_out(ref, sem):
        remote(ref, ref, sem, sem, other).wait_send()


    barrier = pltpu.get_barrier_semaphore()
    each_peer(
        lambda d: pl.semaphore_signal(barrier, inc=1, device_id={"ctx": target(d)}, device_id_type=MESH),
        last_first=True,
        end=NEAR,
    )
    for copy in loads:
        copy.start()

    att = (aq, ak, av)
    for h in range(HEADS):
        for t in range(3):
            pltpu.make_async_copy(
                att[t].at[:, columns(me, h)], qkv.at[h, t, rows(me, ROWS)], qkv_r.at[h, t // 2]
            ).start()

    loads[0].wait()
    loads[1].wait()
    rate = decay[...]
    weight = residue[...]
    for half in range(2):
        cs = slice(half * 128, half * 128 + 128)
        mine[pl.ds(half, MODES, stride=2), :] = jnp.exp(-rate[:, cs])
        mine[pl.ds(STATE + half, MODES, stride=2), :] = weight[:, cs]
        leap[pl.ds(half, MODES, stride=2), :] = jnp.exp(-(rate[:, cs] * float(2 * ROWS)))
    slot = core * CHIPS + chip
    params[rows(slot, 2 * STATE), :] = mine[: 2 * STATE, :]
    loads[2].wait()
    all_in(hx, load_sem.at[3])
    pack_edge(hx, wide)
    edge[...] = wide[:EDGE, :].astype(bf16)

    pl.semaphore_wait(barrier, NEAR - 1)
    pl.semaphore_signal(ready, inc=1, device_id={"ctx": target(N // 2)}, device_id_type=MESH)

    halo_copy = remote(edge, halo, one_s.at[0], one_r.at[0], (me + 1) % N)
    half_rows = CHIPS * 2 * STATE
    par_on = remote(
        params.at[rows(core, half_rows)], params.at[rows(core, half_rows)], one_s.at[1], one_r.at[1], other
    )
    end_on = remote(ends.at[rows(1 - core, CHIPS * STATE)], pair, one_s.at[2], one_r.at[2], other)
    cha_on = remote(beside, carried.at[rows(core, CHIPS * STATE)], one_s.at[3], one_r.at[3], other)

    def par_copy(d, p):
        return remote(
            mine.at[pl.ds(0, 2 * STATE)], params.at[rows(core * CHIPS + p // 2, 2 * STATE)], par_s, par_r, target(d)
        )

    def end_copy(d, p):
        return remote(
            joint.at[rows(target(d) // 2, STATE)], gathered.at[rows(p // 2, STATE)],
            end_s, end_r, target(d),
        )

    def cha_copy(d, p):
        return remote(
            chained.at[rows(target(d) // 2, STATE)], start.at[rows(p // 2, STATE)],
            cha_s, cha_r, target(d),
        )

    def qkv_copy(h, t, d, p):
        return remote(
            att[t].at[:, columns(target(d), h)], qkv.at[h, t, rows(p, ROWS)],
            qkv_s, qkv_r.at[h, t // 2], target(d),
        )

    def mix_copy(h, d, p):
        return remote(
            mixed.at[h, rows(target(d), ROWS)], att_out.at[:, columns(p, h)],
            mix_s, mix_r, target(d),
        )

    def qkv_start(h, tensors, begin=1, end=N):
        def one(d):
            for t in tensors:
                qkv_copy(h, t, d, me).start()

        each_peer(one, last_first=True, begin=begin, end=end)

    each_chip(lambda d: par_copy(d, me).start(), 1, CHIPS // 2 + 1)
    qkv_start(0, (0,), end=NEAR)
    pl.semaphore_wait(ready, 1)
    each_chip(lambda d: par_copy(d, me).start(), CHIPS // 2 + 1, CHIPS)

    @pl.when(me < N - 1)
    def _():
        halo_copy.start()

    qkv_start(0, (0,), begin=NEAR)
    qkv_start(0, (1, 2))
    qkv_start(1, (0,))

    @pl.when(me > 0)
    def _():
        halo_copy.wait_recv()
        wide[:EDGE, :] = halo[...].astype(f32)

    @pl.when(me == 0)
    def _():
        wide[...] = jnp.zeros_like(wide)

    short_filters(hx, wide, taps, qs, product, shifted)
    all_in(params.at[pl.ds(0, (CHIPS - 1) * 2 * STATE)], par_r)
    par_on.start()
    par_on.wait_recv()
    scan(params, product, smooth, ends)
    end_on.start()

    for p in range(CHIPS):
        power = params[pl.ds(pl.multiple_of(core * half_rows + p * 2 * STATE, STATE), STATE), :]
        for _ in range(7):
            power = power * power
        step[p * STATE : (p + 1) * STATE, :] = power

    end_on.wait_recv()
    same = ends[rows(core, CHIPS * STATE), :]
    first = jnp.where(core == 0, same, pair[...])
    joint[...] = first * step[...] + jnp.where(core == 0, pair[...], same)
    gathered[rows(chip, STATE), :] = joint[rows(chip, STATE), :]
    each_chip(lambda d: end_copy(d, me).start())
    qkv_start(1, (1,))
    qkv_start(1, (2,))

    def attention(h):
        all_in(qkv.at[h, pl.ds(0, 2)], qkv_r.at[h, 0])
        for block in range(SEQ // QBLOCK):
            weigh(qkv.at[h, 0], qkv.at[h, 1], weights, sums, block)
        all_in(qkv.at[h, 2], qkv_r.at[h, 1])
        for block in range(SEQ // QBLOCK):
            blend(weights, sums, qkv.at[h, 2], mixed.at[h], block)

    def mix_start(h):
        each_peer(lambda d: mix_copy(h, d, me).start(), last_first=True)
        pltpu.make_async_copy(mixed.at[h, rows(me, ROWS)], att_out.at[:, columns(me, h)], mix_r).start()

    attention(0)

    all_in(gathered.at[pl.ds(0, (CHIPS - 1) * STATE)], end_r)

    def chain(p, state):
        chained[rows(p, STATE), :] = state
        return state * leap[:STATE, :] + gathered[rows(p, STATE), :]

    lax.fori_loop(0, CHIPS, chain, jnp.zeros((STATE, 128), f32))
    start[rows(chip, STATE), :] = chained[rows(chip, STATE), :]
    each_chip(lambda d: cha_copy(d, me).start())

    mix_start(0)

    attention(1)
    mix_start(1)

    all_in(start.at[pl.ds(0, (CHIPS - 1) * STATE)], cha_r)
    same = ends[rows(core, CHIPS * STATE), :]
    first = jnp.where(core == 0, same, pair[...])
    even = start[...]
    odd = even * step[...] + first
    carried[rows(core, CHIPS * STATE), :] = jnp.where(core == 0, even, odd)
    beside[...] = jnp.where(core == 0, odd, even)
    cha_on.start()
    cha_on.wait_recv()
    add_carried(params, carried, smooth)
    gate(smooth, qs, gated)
    last = pltpu.make_async_copy(gated, hyena_out, out_sem)
    last.start()

    @pl.when(me < N - 1)
    def _():
        halo_copy.wait_send()

    for copy in (par_on, end_on, cha_on):
        copy.wait_send()

    all_out(params.at[pl.ds(0, (CHIPS - 1) * 2 * STATE)], par_s)
    all_out(joint.at[pl.ds(0, (CHIPS - 1) * STATE)], end_s)
    all_out(chained.at[pl.ds(0, (CHIPS - 1) * STATE)], cha_s)
    all_out(qkv.at[:, :, pl.ds(0, (N - 1) * ROWS)], qkv_s)
    all_out(mixed.at[:, pl.ds(0, (N - 1) * ROWS)], mix_s)
    all_in(att_out, mix_r)
    last.wait()


PIECES = 4


def hand_over(a_in, b_in, a_out, b_out, room, sem):
    reads, writes = [], []
    for k, (src, dst) in enumerate(((a_in, a_out), (b_in, b_out))):
        for i in range(PIECES):
            piece = pl.ds(i * (ROWS // PIECES), ROWS // PIECES)
            reads.append(pltpu.make_async_copy(src.at[piece], room.at[k, piece], sem.at[0, k, i]))
            writes.append(pltpu.make_async_copy(room.at[k, piece], dst.at[piece], sem.at[1, k, i]))
    for copy in reads:
        copy.start()
    for read, write in zip(reads, writes):
        read.wait()
        write.start()
    for copy in writes:
        copy.wait()


def local(hyena_q, hyena_k, hyena_v, short_filter, residue, decay_rate, att_query, att_key, att_value):
    residue, decay_rate = residue.T, decay_rate.T
    vmem = pltpu.VMEM
    dma = pltpu.SemaphoreType.DMA
    hbm = pl.BlockSpec(memory_space=pltpu.HBM)
    result = jax.ShapeDtypeStruct((ROWS, D), bf16)
    hyena_out, att_out = pl.pallas_call(
        kernel,
        out_shape=(result, result),
        in_specs=[hbm] * 9,
        out_specs=(hbm, hbm),
        scratch_shapes=[
            vmem((3, ROWS, D), bf16),
            vmem(short_filter.shape, f32),
            vmem(residue.shape, f32),
            vmem(decay_rate.shape, f32),
            vmem((EDGE + 8, 128), f32),
            vmem((EDGE, 128), bf16),
            vmem((EDGE, 128), bf16),
            vmem((2 * STATE + 8, 128), f32),
            vmem(((N + 1) * 2 * STATE, 128), f32),
            vmem((STATE + 8, 128), f32),
            vmem((CHIPS * STATE, 128), f32),
            vmem((ROWS, D), f32),
            vmem(((ROWS + 1) * 32, 128), f32),
            vmem(((ROWS + 1) * 32, 128), f32),
            vmem((3, ROWS + 8, 128), f32),
            vmem(((N + 1) * STATE, 128), f32),
            vmem((CHIPS * STATE, 128), f32),
            vmem((CHIPS * STATE, 128), f32),
            vmem((CHIPS * STATE, 128), f32),
            vmem((CHIPS * STATE, 128), f32),
            vmem((CHIPS * STATE, 128), f32),
            vmem((CHIPS * STATE, 128), f32),
            vmem(((N + 1) * STATE, 128), f32),
            vmem((HEADS, 3, SEQ, HEAD), bf16),
            vmem((SEQ, SEQ), bf16),
            vmem((SEQ, HEAD), f32),
            vmem((HEADS, SEQ, HEAD), bf16),
            vmem((ROWS, D), bf16),
            pltpu.SemaphoreType.REGULAR,
            dma((4,)),
            dma,
            dma((4,)),
            dma((4,)),
            dma,
            dma,
            dma,
            dma,
            dma,
            dma,
            dma,
            dma((HEADS, 2)),
            dma,
            dma,
        ],
        compiler_params=pltpu.CompilerParams(
            collective_id=0, has_side_effects=True, vmem_limit_bytes=63 * 2**20
        ),
    )(hyena_q, hyena_k, hyena_v, short_filter, residue, decay_rate, att_query, att_key, att_value)
    return pl.pallas_call(
        hand_over,
        out_shape=(result, result),
        in_specs=[hbm, hbm],
        out_specs=(hbm, hbm),
        scratch_shapes=[vmem((2, ROWS, D), bf16), dma((2, 2, PIECES))],
        compiler_params=pltpu.CompilerParams(vmem_limit_bytes=63 * 2**20),
    )(hyena_out, att_out)


def solution(mesh):
    rows = P(("dp", "ctx"), None)
    placed = (rows, rows, rows, P(), P("ctx", None), P("ctx", None), rows, rows, rows)
    return jax.shard_map(local, mesh=mesh, in_specs=placed, out_specs=(rows, rows), check_vma=False)
```

```python
import functools
import math

import jax
import jax.numpy as jnp
from jax import lax
from jax.experimental import pallas as pl
from jax.experimental.pallas import tpu as pltpu
from jax.sharding import PartitionSpec as P

MESH = pl.DeviceIdType.MESH
f32, bf16 = jnp.float32, jnp.bfloat16

N = 16
CHIPS = N // 2
NEAR = CHIPS + 2
ROWS = 128
SEQ = N * ROWS
D = 4096
MODES = 16
HEAD = 128
HEADS = D // HEAD // N
QBLOCK = 256
EXP2_SCALE = HEAD**-0.5 * math.log2(math.e)
EDGE = 6 * D // 128
STATE = MODES * 2


def row_of(j):
    return j % 2 * 16 + j // 2 % 2 * 8 + j // 4


def total(terms):
    while len(terms) > 1:
        terms = [a + b for a, b in zip(terms[::2], terms[1::2])]
    return terms[0]


def weigh(q_ref, k_ref, weights, sums, block):
    end = (block + 1) * QBLOCK
    start = end - QBLOCK
    scores = lax.dot_general(
        q_ref[start:end, :], k_ref[:end, :], (((1,), (1,)), ((), ())), preferred_element_type=f32
    )
    row = lax.broadcasted_iota(jnp.int32, (QBLOCK, QBLOCK), 0)
    col = lax.broadcasted_iota(jnp.int32, (QBLOCK, QBLOCK), 1)
    diagonal = jnp.where(col <= row, scores[:, start:], -jnp.inf)
    top = jnp.max(diagonal, axis=1, keepdims=True)
    if block:
        top = jnp.maximum(top, jnp.max(scores[:, :start], axis=1, keepdims=True))
        scores = jnp.concatenate([scores[:, :start], diagonal], axis=1)
    else:
        scores = diagonal
    expo = jnp.exp2((scores - top) * EXP2_SCALE)
    sums[start:end, :] = jnp.broadcast_to(jnp.sum(expo, axis=1, keepdims=True), (QBLOCK, HEAD))
    weights[start:end, :end] = expo.astype(bf16)


def blend(weights, sums, v_ref, o_ref, block):
    end = (block + 1) * QBLOCK
    start = end - QBLOCK
    mixed = jnp.dot(weights[start:end, :end], v_ref[:end, :], preferred_element_type=f32)
    o_ref[start:end, :] = (mixed / sums[start:end, :]).astype(bf16)


def edge_at(j, f, r):
    return pl.ds(j * 6 + 2 * f + r, 1)


def pack_edge(hx, wide):
    def column(j, carry):
        cs = pl.ds(pl.multiple_of(j * 128, 128), 128)
        for f in range(3):
            last = hx[f, ROWS - 16 : ROWS, cs].astype(f32)
            for r in range(2):
                wide[edge_at(j, f, r), :] = last[14 + r : 15 + r]
        return carry

    lax.fori_loop(0, D // 128, column, 0)


def short_filters(hx, halo, taps, qs, product, shifted):
    def column(j, carry):
        cs = pl.ds(pl.multiple_of(j * 128, 128), 128)

        def mix(f):
            x = hx[f, :, cs].astype(f32)
            shifted[f, 8 : 8 + ROWS, :] = x
            for r in range(2):
                shifted[f, 6 + r : 7 + r, :] = halo[edge_at(j, f, r), :]
            w = taps[f, :, cs]
            return (
                w[0:1] * x + w[1:2] * shifted[f, 7 : 7 + ROWS, :] + w[2:3] * shifted[f, 6 : 6 + ROWS, :]
            )

        qs[:, cs] = mix(0)
        both = (mix(1) * mix(2)).astype(bf16).astype(f32)
        product[pl.ds(row_of(j), ROWS, stride=32), :] = both
        return carry

    lax.fori_loop(0, D // 128, column, 0)


def mode_rows(ref, g, n, per_owner, first=0):
    return pl.ds(g % 2 * 8 * per_owner + first + n * 2 + g // 2, 8, stride=per_owner)


def scan(params, product, smooth, states):
    for g in range(4):
        power = [params[mode_rows(params, g, n, 2 * STATE), :] for n in range(MODES)]
        weight = [params[mode_rows(params, g, n, 2 * STATE, STATE), :] for n in range(MODES)]

        def step(t, state):
            rows = pl.ds(pl.multiple_of(t * 32 + g * 8, 8), 8)
            x = product[rows, :]
            state = [h * p + x for h, p in zip(state, power)]
            smooth[rows, :] = total([h * w for h, w in zip(state, weight)])
            return state

        state = lax.fori_loop(0, ROWS, step, [jnp.zeros((8, 128), f32)] * MODES, unroll=4)
        for n in range(MODES):
            states[mode_rows(states, g, n, STATE), :] = state[n]


def add_carried(params, carried, smooth):
    for g in range(4):
        power = [params[mode_rows(params, g, n, 2 * STATE), :] for n in range(MODES)]
        first = [
            params[mode_rows(params, g, n, 2 * STATE, STATE), :]
            * power[n]
            * carried[mode_rows(carried, g, n, STATE), :]
            for n in range(MODES)
        ]

        def step(t, term):
            rows = pl.ds(pl.multiple_of(t * 32 + g * 8, 8), 8)
            smooth[rows, :] = smooth[rows, :] + total(term)
            return [a * p for a, p in zip(term, power)]

        lax.fori_loop(0, ROWS, step, first, unroll=4)


def gate(smooth, qs, out):
    def column(j, carry):
        cs = pl.ds(pl.multiple_of(j * 128, 128), 128)
        y = smooth[pl.ds(row_of(j), ROWS, stride=32), :]
        out[:, cs] = (qs[:, cs] * y.astype(bf16).astype(f32)).astype(bf16)
        return carry

    lax.fori_loop(0, D // 128, column, 0, unroll=4)


def kernel(
    hq, hk, hv, taps_in, residue_in, decay_in, aq, ak, av,
    hyena_out, att_out,
    hx, taps, residue, decay, wide, edge, halo, mine, params, leap, step, qs, product, smooth, shifted,
    ends, pair, joint, gathered, chained, start, beside, carried, qkv, weights, sums, mixed, gated,
    ready, load_sem, out_sem, one_s, one_r,
    par_s, par_r, end_s, end_r, cha_s, cha_r, qkv_s, qkv_r, mix_s, mix_r,
):
    me = lax.axis_index("ctx")
    core = me % 2
    chip = me // 2
    other = me + 1 - 2 * core

    def target(d):
        z = (chip + d // 2) % 4
        return (me // 8 + d // 8) % 2 * 8 + z * 2 + (me + d) % 2

    def each_peer(do, last_first=False, begin=1, end=N):
        def at(d, carry):
            do(begin + end - 1 - d if last_first else d)
            return carry

        lax.fori_loop(begin, end, at, 0)

    def each_chip(do, begin=1, end=CHIPS):
        def at(e, carry):
            do(2 * e)
            return carry

        lax.fori_loop(begin, end, at, 0)

    def rows(p, count):
        return pl.ds(pl.multiple_of(p * count, count), count)

    def columns(p, h):
        return pl.ds(pl.multiple_of((p * HEADS + h) * HEAD, HEAD), HEAD)

    def remote(src, dst, send, recv, device):
        return pltpu.make_async_remote_copy(
            src_ref=src, dst_ref=dst, send_sem=send, recv_sem=recv,
            device_id={"ctx": device}, device_id_type=MESH,
        )

    loads = [
        pltpu.make_async_copy(src, dst, load_sem.at[min(i, 3)])
        for i, (src, dst) in enumerate(
            [(residue_in, residue), (decay_in, decay), (taps_in, taps)]
            + [(x, hx.at[f]) for f, x in enumerate((hq, hk, hv))]
        )
    ]

    def all_in(ref, sem):
        pltpu.make_async_copy(ref, ref, sem).wait()

    def all_out(ref, sem):
        remote(ref, ref, sem, sem, other).wait_send()


    barrier = pltpu.get_barrier_semaphore()
    each_peer(
        lambda d: pl.semaphore_signal(barrier, inc=1, device_id={"ctx": target(d)}, device_id_type=MESH),
        last_first=True,
        end=NEAR,
    )
    for copy in loads:
        copy.start()

    att = (aq, ak, av)
    for h in range(HEADS):
        for t in range(3):
            pltpu.make_async_copy(
                att[t].at[:, columns(me, h)], qkv.at[h, t, rows(me, ROWS)], qkv_r.at[h, t // 2]
            ).start()

    loads[0].wait()
    loads[1].wait()
    rate = decay[...]
    weight = residue[...]
    for half in range(2):
        cs = slice(half * 128, half * 128 + 128)
        mine[pl.ds(half, MODES, stride=2), :] = jnp.exp(-rate[:, cs])
        mine[pl.ds(STATE + half, MODES, stride=2), :] = weight[:, cs]
        leap[pl.ds(half, MODES, stride=2), :] = jnp.exp(-(rate[:, cs] * float(2 * ROWS)))
    slot = core * CHIPS + chip
    params[rows(slot, 2 * STATE), :] = mine[: 2 * STATE, :]

    pl.semaphore_wait(barrier, NEAR - 1)
    pl.semaphore_signal(ready, inc=1, device_id={"ctx": target(N // 2)}, device_id_type=MESH)

    halo_copy = remote(edge, halo, one_s.at[0], one_r.at[0], (me + 1) % N)
    half_rows = CHIPS * 2 * STATE
    par_on = remote(
        params.at[rows(core, half_rows)], params.at[rows(core, half_rows)], one_s.at[1], one_r.at[1], other
    )
    end_on = remote(ends.at[rows(1 - core, CHIPS * STATE)], pair, one_s.at[2], one_r.at[2], other)
    cha_on = remote(beside, carried.at[rows(core, CHIPS * STATE)], one_s.at[3], one_r.at[3], other)

    def par_copy(d, p):
        return remote(
            mine.at[pl.ds(0, 2 * STATE)], params.at[rows(core * CHIPS + p // 2, 2 * STATE)], par_s, par_r, target(d)
        )

    def end_copy(d, p):
        return remote(
            joint.at[rows(target(d) // 2, STATE)], gathered.at[rows(p // 2, STATE)],
            end_s, end_r, target(d),
        )

    def cha_copy(d, p):
        return remote(
            chained.at[rows(target(d) // 2, STATE)], start.at[rows(p // 2, STATE)],
            cha_s, cha_r, target(d),
        )

    def qkv_copy(h, t, d, p):
        return remote(
            att[t].at[:, columns(target(d), h)], qkv.at[h, t, rows(p, ROWS)],
            qkv_s, qkv_r.at[h, t // 2], target(d),
        )

    def mix_copy(h, d, p):
        return remote(
            mixed.at[h, rows(target(d), ROWS)], att_out.at[:, columns(p, h)],
            mix_s, mix_r, target(d),
        )

    def qkv_start(h, tensors, begin=1, end=N):
        def one(d):
            for t in tensors:
                qkv_copy(h, t, d, me).start()

        each_peer(one, last_first=True, begin=begin, end=end)

    each_chip(lambda d: par_copy(d, me).start(), 1, CHIPS // 2 + 1)
    qkv_start(0, (0,), end=NEAR)
    loads[2].wait()
    all_in(hx, load_sem.at[3])
    pack_edge(hx, wide)
    edge[...] = wide[:EDGE, :].astype(bf16)
    pl.semaphore_wait(ready, 1)
    each_chip(lambda d: par_copy(d, me).start(), CHIPS // 2 + 1, CHIPS)

    @pl.when(me < N - 1)
    def _():
        halo_copy.start()

    qkv_start(0, (0,), begin=NEAR)
    qkv_start(0, (1, 2))
    qkv_start(1, (0,))

    @pl.when(me > 0)
    def _():
        halo_copy.wait_recv()
        wide[:EDGE, :] = halo[...].astype(f32)

    @pl.when(me == 0)
    def _():
        wide[...] = jnp.zeros_like(wide)

    short_filters(hx, wide, taps, qs, product, shifted)
    all_in(params.at[pl.ds(0, (CHIPS - 1) * 2 * STATE)], par_r)
    par_on.start()
    par_on.wait_recv()
    scan(params, product, smooth, ends)
    end_on.start()

    for p in range(CHIPS):
        power = params[pl.ds(pl.multiple_of(core * half_rows + p * 2 * STATE, STATE), STATE), :]
        for _ in range(7):
            power = power * power
        step[p * STATE : (p + 1) * STATE, :] = power

    end_on.wait_recv()
    same = ends[rows(core, CHIPS * STATE), :]
    first = jnp.where(core == 0, same, pair[...])
    joint[...] = first * step[...] + jnp.where(core == 0, pair[...], same)
    gathered[rows(chip, STATE), :] = joint[rows(chip, STATE), :]
    each_chip(lambda d: end_copy(d, me).start())
    qkv_start(1, (1,))
    qkv_start(1, (2,))

    def attention(h):
        all_in(qkv.at[h, pl.ds(0, 2)], qkv_r.at[h, 0])
        for block in range(SEQ // QBLOCK):
            weigh(qkv.at[h, 0], qkv.at[h, 1], weights, sums, block)
        all_in(qkv.at[h, 2], qkv_r.at[h, 1])
        for block in range(SEQ // QBLOCK):
            blend(weights, sums, qkv.at[h, 2], mixed.at[h], block)

    def mix_start(h):
        each_peer(lambda d: mix_copy(h, d, me).start(), last_first=True)
        pltpu.make_async_copy(mixed.at[h, rows(me, ROWS)], att_out.at[:, columns(me, h)], mix_r).start()

    attention(0)

    all_in(gathered.at[pl.ds(0, (CHIPS - 1) * STATE)], end_r)

    def chain(p, state):
        chained[rows(p, STATE), :] = state
        return state * leap[:STATE, :] + gathered[rows(p, STATE), :]

    lax.fori_loop(0, CHIPS, chain, jnp.zeros((STATE, 128), f32))
    start[rows(chip, STATE), :] = chained[rows(chip, STATE), :]
    each_chip(lambda d: cha_copy(d, me).start())

    mix_start(0)

    attention(1)
    mix_start(1)

    all_in(start.at[pl.ds(0, (CHIPS - 1) * STATE)], cha_r)
    same = ends[rows(core, CHIPS * STATE), :]
    first = jnp.where(core == 0, same, pair[...])
    even = start[...]
    odd = even * step[...] + first
    carried[rows(core, CHIPS * STATE), :] = jnp.where(core == 0, even, odd)
    beside[...] = jnp.where(core == 0, odd, even)
    cha_on.start()
    cha_on.wait_recv()
    add_carried(params, carried, smooth)
    gate(smooth, qs, gated)
    last = pltpu.make_async_copy(gated, hyena_out, out_sem)
    last.start()

    @pl.when(me < N - 1)
    def _():
        halo_copy.wait_send()

    for copy in (par_on, end_on, cha_on):
        copy.wait_send()

    all_out(params.at[pl.ds(0, (CHIPS - 1) * 2 * STATE)], par_s)
    all_out(joint.at[pl.ds(0, (CHIPS - 1) * STATE)], end_s)
    all_out(chained.at[pl.ds(0, (CHIPS - 1) * STATE)], cha_s)
    all_out(qkv.at[:, :, pl.ds(0, (N - 1) * ROWS)], qkv_s)
    all_out(mixed.at[:, pl.ds(0, (N - 1) * ROWS)], mix_s)
    all_in(att_out, mix_r)
    last.wait()


PIECES = 4


def hand_over(a_in, b_in, a_out, b_out, room, sem):
    reads, writes = [], []
    for k, (src, dst) in enumerate(((a_in, a_out), (b_in, b_out))):
        for i in range(PIECES):
            piece = pl.ds(i * (ROWS // PIECES), ROWS // PIECES)
            reads.append(pltpu.make_async_copy(src.at[piece], room.at[k, piece], sem.at[0, k, i]))
            writes.append(pltpu.make_async_copy(room.at[k, piece], dst.at[piece], sem.at[1, k, i]))
    for copy in reads:
        copy.start()
    for read, write in zip(reads, writes):
        read.wait()
        write.start()
    for copy in writes:
        copy.wait()


def local(hyena_q, hyena_k, hyena_v, short_filter, residue, decay_rate, att_query, att_key, att_value):
    residue, decay_rate = residue.T, decay_rate.T
    vmem = pltpu.VMEM
    dma = pltpu.SemaphoreType.DMA
    hbm = pl.BlockSpec(memory_space=pltpu.HBM)
    result = jax.ShapeDtypeStruct((ROWS, D), bf16)
    hyena_out, att_out = pl.pallas_call(
        kernel,
        out_shape=(result, result),
        in_specs=[hbm] * 9,
        out_specs=(hbm, hbm),
        scratch_shapes=[
            vmem((3, ROWS, D), bf16),
            vmem(short_filter.shape, f32),
            vmem(residue.shape, f32),
            vmem(decay_rate.shape, f32),
            vmem((EDGE + 8, 128), f32),
            vmem((EDGE, 128), bf16),
            vmem((EDGE, 128), bf16),
            vmem((2 * STATE + 8, 128), f32),
            vmem(((N + 1) * 2 * STATE, 128), f32),
            vmem((STATE + 8, 128), f32),
            vmem((CHIPS * STATE, 128), f32),
            vmem((ROWS, D), f32),
            vmem(((ROWS + 1) * 32, 128), f32),
            vmem(((ROWS + 1) * 32, 128), f32),
            vmem((3, ROWS + 8, 128), f32),
            vmem(((N + 1) * STATE, 128), f32),
            vmem((CHIPS * STATE, 128), f32),
            vmem((CHIPS * STATE, 128), f32),
            vmem((CHIPS * STATE, 128), f32),
            vmem((CHIPS * STATE, 128), f32),
            vmem((CHIPS * STATE, 128), f32),
            vmem((CHIPS * STATE, 128), f32),
            vmem(((N + 1) * STATE, 128), f32),
            vmem((HEADS, 3, SEQ, HEAD), bf16),
            vmem((SEQ, SEQ), bf16),
            vmem((SEQ, HEAD), f32),
            vmem((HEADS, SEQ, HEAD), bf16),
            vmem((ROWS, D), bf16),
            pltpu.SemaphoreType.REGULAR,
            dma((4,)),
            dma,
            dma((4,)),
            dma((4,)),
            dma,
            dma,
            dma,
            dma,
            dma,
            dma,
            dma,
            dma((HEADS, 2)),
            dma,
            dma,
        ],
        compiler_params=pltpu.CompilerParams(
            collective_id=0, has_side_effects=True, vmem_limit_bytes=63 * 2**20
        ),
    )(hyena_q, hyena_k, hyena_v, short_filter, residue, decay_rate, att_query, att_key, att_value)
    return pl.pallas_call(
        hand_over,
        out_shape=(result, result),
        in_specs=[hbm, hbm],
        out_specs=(hbm, hbm),
        scratch_shapes=[vmem((2, ROWS, D), bf16), dma((2, 2, PIECES))],
        compiler_params=pltpu.CompilerParams(vmem_limit_bytes=63 * 2**20),
    )(hyena_out, att_out)


def solution(mesh):
    rows = P(("dp", "ctx"), None)
    placed = (rows, rows, rows, P(), P("ctx", None), P("ctx", None), rows, rows, rows)
    return jax.shard_map(local, mesh=mesh, in_specs=placed, out_specs=(rows, rows), check_vma=False)
```
